512 devices in a mesh: section: 4 (over z_lo), group: 16 (over x, y), tensor: 8 (over z_hi, core).
Axes of the slice: x: 4, y: 4, z: 16 (z_hi: 4, z_lo: 4; z = z_hi * 4 + z_lo), core: 2. Of those that a mesh axis runs over, the one named last changes fastest.
Arguments:
- x_pre: bfloat16 [1024, 32, 8192], P(('section', 'group'), None, 'tensor'), may hold values from -6 to 6
- z_pre: bfloat16 [1024, 32, 8192], P(('section', 'group'), None, 'tensor'), may hold values from -6 to 6
- b_pre: bfloat16 [1024, 32, 16], P(('section', 'group')), may hold values from -4 to 4
- c_pre: bfloat16 [1024, 32, 16], P(('section', 'group')), may hold values from -4 to 4
- dt_pre: float32 [1024, 32, 128], P(('section', 'group'), None, 'tensor'), may hold values from -6 to 6
- lengths: int32 [1024], P(('section', 'group')), may hold values from 1 to 32, as said below
- owner: int32 [1024], replicated, may hold values from 0 to 15, as said below
- dec_x: bfloat16 [1024, 4, 8192], P(('section', 'group'), None, 'tensor'), may hold values from -6 to 6
- dec_z: bfloat16 [1024, 4, 8192], P(('section', 'group'), None, 'tensor'), may hold values from -6 to 6
- dec_b: bfloat16 [1024, 4, 16], P(('section', 'group')), may hold values from -4 to 4
- dec_c: bfloat16 [1024, 4, 16], P(('section', 'group')), may hold values from -4 to 4
- dec_dt: float32 [1024, 4, 128], P(('section', 'group'), None, 'tensor'), may hold values from -6 to 6
- decay_rate: float32 [128], P('tensor'), may hold values from 0.002 to 0.05
- dt_bias: float32 [128], P('tensor'), may hold values from -1 to 1
- skip: float32 [128], P('tensor'), may hold values from 0.5 to 1.5
- norm_gain: float32 [8192], P('tensor'), may hold values from 0.5 to 1.5
Outputs:
- pre_out: bfloat16 [1024, 32, 8192], P(('section', 'group'), None, 'tensor')
- dec_out: bfloat16 [1024, 4, 8192], P(('section', 'group'), None, 'tensor')
- dec_state: float32 [1024, 16, 8192], P(('section', 'group'), None, 'tensor')
The draws below stay inside these ranges and needn't reach their ends.
Inputs may be any that keep to these rules, and one draw needn't show every extreme that they name: `lengths`: each request has 1 to 32 new tokens; in each aligned block of 16 requests (one cell) one request has exactly 32. owner[r] is the group, within the next pool along the section axis, of request r's decode owner. The 16 requests of one cell go exactly 2 each to half of the groups; each group of a pool receives exactly 16 requests from the previous pool.
All inputs are finite; a program needn't handle non-finite values.
Results may differ from the reference program's by a relative error of at most 0.0012.
Values sent between devices are 32-bit elements; how exact they have to be, the bound alone decides.
A program may use at most 64 MiB of HBM per device.

```python
import math
import jax
import jax.numpy as jnp
from jax import lax

STATE = 16
CHAN = 8192
HEAD = 64
LEN = 32
REQ_DEV = 16
STEPS = 4
PAIR = 2
HEADS = 128
CELLS = 64
REQS = 1024
SLOT_DEV = 16
SLOTS = 1024
N_SECTION = 4
N_GROUP = 16


def draw_lengths(key, part):
    key = jax.random.fold_in(key, 11)
    first_key, second_key = jax.random.split(key)
    counts = jax.random.randint(first_key, (CELLS, REQ_DEV), 1, LEN + 1)
    full_at = jax.random.randint(second_key, (CELLS,), 0, REQ_DEV)
    counts = jnp.where(jnp.arange(REQ_DEV)[None, :] == full_at[:, None], LEN, counts)
    return counts.reshape(REQS).astype(jnp.int32)


def owners_of_section(section_key):
    first_key, second_key, third_key = jax.random.split(section_key, 3)
    offsets = jax.random.permutation(first_key, N_GROUP)[:N_GROUP // 2]
    relabel = jax.random.permutation(second_key, N_GROUP)
    sources = jnp.arange(N_GROUP)
    targets = relabel[(sources[:, None] + offsets[None, :]) % N_GROUP]
    owners = jnp.repeat(targets, PAIR, axis=1)
    orders = jax.vmap(lambda row_key: jax.random.permutation(row_key, REQ_DEV))(jax.random.split(third_key, N_GROUP))
    return jnp.take_along_axis(owners, orders, axis=1)


def draw_owner(key, part):
    key = jax.random.fold_in(key, 23)
    owners = jax.vmap(owners_of_section)(jax.random.split(key, N_SECTION))
    return owners.reshape(REQS).astype(jnp.int32)


def level_of(key, dims, cuts, low, high):
    loudness, own = 1.0, jax.random.fold_in(key, 6)
    for dim, shards_of in cuts:
        draws = jnp.exp(jax.random.uniform(jax.random.fold_in(own, dim), (shards_of,), jnp.float32, low / len(cuts), high / len(cuts)))
        loudness = loudness * jnp.repeat(draws, dims[dim] // shards_of).reshape([-1 if axis == dim else 1 for axis in range(len(dims))])
    return loudness


def centred(key, dims, width, most, cuts=(), held_as=jnp.bfloat16):
    result = width * jax.random.normal(key, dims, jnp.float32)
    if cuts:
        result = result * level_of(key, dims, cuts, -0.22, 0.18)
    return jnp.clip(result, -most, most).astype(held_as)


def setup_inputs(seed: int = 0) -> dict:
    seeds = jax.random.split(jax.random.key(seed), 17)
    return {
        "x_pre": centred(seeds[0], (REQS, LEN, CHAN), 1.0, 6.0, ((0, 64), (2, 8))),
        "z_pre": centred(seeds[1], (REQS, LEN, CHAN), 1.0, 6.0, ((0, 64), (2, 8))),
        "b_pre": centred(seeds[2], (REQS, LEN, STATE), 0.5, 4.0, ((0, 64),)),
        "c_pre": centred(seeds[3], (REQS, LEN, STATE), 0.5, 4.0, ((0, 64),)),
        "dt_pre": centred(seeds[4], (REQS, LEN, HEADS), 1.0, 6.0, ((0, 64), (2, 8)), jnp.float32),
        "lengths": draw_lengths(jax.random.fold_in(seeds[16], 71), 0),
        "owner": draw_owner(jax.random.fold_in(seeds[16], 71), 0),
        "dec_x": centred(seeds[7], (SLOTS, STEPS, CHAN), 1.0, 6.0, ((0, 64), (2, 8))),
        "dec_z": centred(seeds[8], (SLOTS, STEPS, CHAN), 1.0, 6.0, ((0, 64), (2, 8))),
        "dec_b": centred(seeds[9], (SLOTS, STEPS, STATE), 0.5, 4.0, ((0, 64),)),
        "dec_c": centred(seeds[10], (SLOTS, STEPS, STATE), 0.5, 4.0, ((0, 64),)),
        "dec_dt": centred(seeds[11], (SLOTS, STEPS, HEADS), 1.0, 6.0, ((0, 64), (2, 8)), jnp.float32),
        "decay_rate": jnp.clip(jnp.exp(math.log(0.05) - 3.218876 * jax.random.uniform(seeds[12], (HEADS,), jnp.float32) ** level_of(seeds[12], (HEADS,), ((0, 8),), -0.2, 0.2)), 0.002, 0.05),
        "dt_bias": jnp.clip(jax.random.uniform(seeds[13], (HEADS,), jnp.float32, -1.0, 1.0) * level_of(seeds[13], (HEADS,), ((0, 8),), -0.4, 0.0), -1.0, 1.0),
        "skip": jnp.clip(0.5 + 1.0 * jax.random.uniform(seeds[14], (HEADS,), jnp.float32) ** level_of(seeds[14], (HEADS,), ((0, 8),), -0.2, 0.2), 0.5, 1.5),
        "norm_gain": jnp.clip(1.0 + 0.1 * jax.random.normal(seeds[15], (CHAN,), jnp.float32), 0.5, 1.5),
    }


EPS = 1e-05

def per_channel(values, head_size):
    return jnp.broadcast_to(values[..., None], values.shape + (head_size,)).reshape(values.shape[:-1] + (values.shape[-1] * head_size,))

def recurrence(carry_state, x_step, z_step, b_step, c_step, dt_step, live_mask, decay_rate, dt_bias, skip_chan, norm_gain):
    step_size = jax.nn.softplus(dt_step + dt_bias) * live_mask[:, None]
    decay_step = per_channel(jnp.exp(-decay_rate * step_size), HEAD)
    x_float = x_step.astype(jnp.float32)
    inject = per_channel(step_size, HEAD) * x_float
    carry_state = carry_state * decay_step[:, None, :] + b_step.astype(jnp.float32)[:, :, None] * inject[:, None, :]
    mixed = lax.optimization_barrier(jnp.sum(carry_state * c_step.astype(jnp.float32)[:, :, None], axis=1)) + skip_chan * x_float
    gated_out = mixed * jax.nn.silu(z_step.astype(jnp.float32))
    sq_total = lax.optimization_barrier(jnp.sum(gated_out * gated_out, axis=1))
    normed = gated_out * lax.rsqrt(sq_total / CHAN + EPS)[:, None] * norm_gain * live_mask[:, None]
    return (carry_state, normed.astype(jnp.bfloat16))

def reference(x_pre, z_pre, b_pre, c_pre, dt_pre, lengths, owner, dec_x, dec_z, dec_b, dec_c, dec_dt, decay_rate, dt_bias, skip, norm_gain):
    cell_count = N_SECTION * N_GROUP
    skip_chan = per_channel(skip, HEAD)

    def prefill(block_args):
        x_cell, z_cell, b_cell, c_cell, dt_cell, length_cell = block_args

        def advance(carry_state, position):
            live_mask = (position < length_cell).astype(jnp.float32)
            return recurrence(carry_state, x_cell[:, position], z_cell[:, position], b_cell[:, position], c_cell[:, position], dt_cell[:, position], live_mask, decay_rate, dt_bias, skip_chan, norm_gain)
        initial = jnp.zeros((REQ_DEV, STATE, CHAN), jnp.float32)
        final_state, step_outs = lax.scan(advance, initial, jnp.arange(LEN, dtype=jnp.int32))
        return (final_state, jnp.swapaxes(step_outs, 0, 1))
    finals, pre_out = lax.map(prefill, (x_pre.reshape(cell_count, REQ_DEV, LEN, CHAN), z_pre.reshape(cell_count, REQ_DEV, LEN, CHAN), b_pre.reshape(cell_count, REQ_DEV, LEN, STATE), c_pre.reshape(cell_count, REQ_DEV, LEN, STATE), dt_pre.reshape(cell_count, REQ_DEV, LEN, HEADS), lengths.reshape(cell_count, REQ_DEV)))
    finals = finals.reshape(REQS, STATE, CHAN)
    pre_out = pre_out.reshape(REQS, LEN, CHAN)
    per_section = N_GROUP * REQ_DEV
    owner_section = owner.reshape(N_SECTION, per_section)
    section_index = jnp.arange(per_section, dtype=jnp.int32)
    same_owner = owner_section[:, :, None] == owner_section[:, None, :]
    earlier = section_index[None, :] < section_index[:, None]
    rank = lax.optimization_barrier(jnp.sum((same_owner & earlier[None, :, :]).astype(jnp.int32), axis=2)).astype(jnp.int32)
    section_ids = jnp.arange(N_SECTION, dtype=jnp.int32)
    dest_cell = ((section_ids + 1) % N_SECTION)[:, None] * N_GROUP + owner_section
    slot_index = (dest_cell * SLOT_DEV + rank).reshape(-1).astype(jnp.int32)
    source_of = jnp.zeros((SLOTS,), jnp.int32).at[slot_index].set(jnp.arange(REQS, dtype=jnp.int32))

    def decode(block_args):
        source, x_steps, z_steps, b_steps, c_steps, dt_steps = block_args
        carry_state = jnp.take(finals, source, axis=0)
        live_mask = jnp.ones((SLOT_DEV,), jnp.float32)
        outputs = []
        for step_index in range(STEPS):
            carry_state, normed = recurrence(carry_state, x_steps[:, step_index], z_steps[:, step_index], b_steps[:, step_index], c_steps[:, step_index], dt_steps[:, step_index], live_mask, decay_rate, dt_bias, skip_chan, norm_gain)
            outputs.append(normed)
        return (jnp.stack(outputs, axis=1), carry_state)
    dec_out, dec_state = lax.map(decode, (source_of.reshape(cell_count, SLOT_DEV), dec_x.reshape(cell_count, SLOT_DEV, STEPS, CHAN), dec_z.reshape(cell_count, SLOT_DEV, STEPS, CHAN), dec_b.reshape(cell_count, SLOT_DEV, STEPS, STATE), dec_c.reshape(cell_count, SLOT_DEV, STEPS, STATE), dec_dt.reshape(cell_count, SLOT_DEV, STEPS, HEADS)))
    return (pre_out, dec_out.reshape(SLOTS, STEPS, CHAN), dec_state.reshape(SLOTS, STATE, CHAN))
```

```python
import functools

import jax
import jax.numpy as jnp
from jax import lax
from jax.experimental import pallas as pl
from jax.experimental.pallas import tpu as pltpu
from jax.sharding import PartitionSpec as P

CHAN = 8192
EPS = 1e-05
MESH = pl.DeviceIdType.MESH
F32 = jnp.float32
BF16 = jnp.bfloat16

REQ = 16
LEN = 32
STATE = 16
HEADS = 16
WIDTH = 1024
STEPS = 4
SIDE = 4
GROUPS = 16
SECTIONS = 4
TENSORS = 8
PARTS = 8
PART = WIDTH // PARTS
BLOCK = 256


def iota(shape, dim):
    return lax.broadcasted_iota(jnp.int32, shape, dim)


def softplus(v):
    return jnp.maximum(v, 0.0) + jnp.log1p(jnp.exp(-jnp.abs(v)))


def silu(v):
    return v / (1.0 + jnp.exp(-v))


def two_terms(v):
    high = v.astype(BF16)
    return high, (v - high.astype(F32)).astype(BF16)


def three_terms(v):
    high = v.astype(BF16)
    rest = v - high.astype(F32)
    mid = rest.astype(BF16)
    return high, mid, (rest - mid.astype(F32)).astype(BF16)


def dot(a, b):
    return jnp.dot(a, b, preferred_element_type=F32)


def from_scalars(ref, where_index, count):
    acc = jnp.zeros(where_index.shape, ref.dtype)
    for k in range(count):
        acc = jnp.where(where_index == k, ref[k], acc)
    return acc


def kernel(
    lengths, owner, rate, bias, skip,
    b_t, c_t, dt_t, dec_x, dec_z, dec_b, dec_c, dec_dt, gain,
    x_hbm, z_hbm,
    pre_hbm, dec_hbm, state_hbm,
    *scratch,
):
    (x_v, z_v, turn, lhs, expand_lhs, mixed, squares, z_send, x_send, staged, pre_v,
     dec_v, dec_decay, dec_inject, dec_skip, dec_gate, dec_cols, dec_gated, dec_squares,
     pack, got, source, rows, local_sem, z_sem, x_sem, t_sem) = scratch[:27]
    z_recv = scratch[27:27 + PARTS]
    x_recv = scratch[27 + PARTS:27 + 2 * PARTS]

    section = lax.axis_index("section")
    group = lax.axis_index("group")
    tensor = lax.axis_index("tensor")
    gx, gy = group // SIDE, lax.rem(group, SIDE)
    ahead = lax.rem(section + 1, SECTIONS)
    behind = lax.rem(section + SECTIONS - 1, SECTIONS)

    def group_at(d):
        return lax.rem(gx + d // SIDE, SIDE) * SIDE + lax.rem(gy + lax.rem(d, SIDE), SIDE)

    blocks = WIDTH // BLOCK
    x_copies = []
    for k in range(blocks):
        cols = pl.ds(k * BLOCK, BLOCK)
        copy = pltpu.make_async_copy(x_hbm.at[:, :, cols], x_v.at[:, :, cols], local_sem.at[k])
        copy.start()
        x_copies.append(copy)
    z_copy = pltpu.make_async_copy(z_hbm, z_v, local_sem.at[blocks])
    z_copy.start()

    barrier = pltpu.get_barrier_semaphore()
    for to in (ahead, behind):
        pl.semaphore_signal(barrier, inc=1, device_id=(to, group, tensor), device_id_type=MESH)
    for d in range(1, GROUPS):
        pl.semaphore_signal(barrier, inc=1, device_id=(section, group_at(d), tensor), device_id_type=MESH)
    for d in range(1, TENSORS):
        pl.semaphore_signal(
            barrier, inc=1, device_id=(section, group, lax.rem(tensor + d, TENSORS)), device_id_type=MESH
        )

    turn[...] = jnp.zeros_like(turn)
    turn[:, 0:LEN] = dt_t[...].reshape(REQ * HEADS, LEN)
    logits = jnp.transpose(turn[...])[0:LEN]
    lane = iota((1, REQ * HEADS), 1)
    head_of, req_of = lax.rem(lane, HEADS), lane // HEADS
    live = iota((LEN, REQ * HEADS), 0) < from_scalars(lengths, req_of, REQ)
    step = jnp.where(live, softplus(logits + from_scalars(bias, head_of, HEADS)), 0.0)
    fall = from_scalars(rate, head_of, HEADS) * step
    lower = (iota((LEN, LEN), 0) >= iota((LEN, LEN), 1)).astype(F32).astype(BF16)
    total = sum(dot(lower, term) for term in three_terms(fall))
    shrink = jnp.exp(-total)
    grow = jnp.exp(total) * step

    turn[:, 0:LEN] = c_t[...].reshape(REQ * STATE, LEN).astype(F32)
    c_tok = jnp.transpose(turn[...])[0:LEN]
    spread = (lax.rem(iota((LEN, 3 * LEN), 1), LEN) == iota((LEN, 3 * LEN), 0)).astype(F32).astype(BF16)
    b_rep = dot(b_t[...].reshape(REQ * STATE, LEN), spread)
    lane3 = iota((LEN, 3 * LEN), 1)
    middle = (lane3 >= LEN) & (lane3 < 2 * LEN)
    causal = iota((LEN, 3 * LEN), 0) >= lax.rem(lane3, LEN)
    lane128 = iota((LEN, 128), 1) // HEADS
    half_reqs = 128 // HEADS
    for r in range(REQ):
        half = slice((r // half_reqs) * 128, (r // half_reqs) * 128 + 128)
        mine = lane128 == r % half_reqs
        for at, values in ((0, grow), (LEN, shrink)):
            high, low = two_terms(jnp.where(mine, values[:, half], 0.0))
            expand_lhs[r, at:at + LEN, 0:128] = high
            expand_lhs[r, at:at + LEN, 128:256] = low
        gram = dot(jnp.where(mine, c_tok[:, half], 0.0).astype(BF16), b_rep[half].astype(BF16))
        high = gram.astype(BF16).astype(F32)
        lhs[r, 0:LEN, :] = jnp.where(causal, jnp.where(middle, gram - high, high), 0.0).astype(BF16)
        lhs[r, LEN:LEN + STATE, :] = jnp.where(
            middle[0:STATE], 0.0, b_rep[r * STATE:(r + 1) * STATE]
        ).astype(BF16)

    z_out = []
    for k in range(blocks):
        x_copies[k].wait()
        cols = slice(k * BLOCK, (k + 1) * BLOCK)
        head_rows = lax.rem(iota((256, BLOCK), 0), HEADS)
        head_cols = iota((256, BLOCK), 1) // 64 + k * (BLOCK // 64)
        expand = (head_rows == head_cols).astype(F32).astype(BF16)
        skip_row = from_scalars(skip, iota((1, BLOCK), 1) // 64 + k * (BLOCK // 64), HEADS)

        def prefill(i, _, k=k, cols=cols, expand=expand, skip_row=skip_row):
            for sub in range(4):
                r = i * 4 + sub
                wide = dot(expand_lhs[r], expand)
                x_f = x_v[r, :, cols].astype(F32)
                high, low = two_terms(x_f * wide[0:LEN])
                res = dot(lhs[r], jnp.concatenate([high, high, low], axis=0))
                mixed[r, :, cols] = res[0:LEN] * wide[LEN:2 * LEN] + skip_row * x_f
                final = res[LEN:LEN + STATE] * wide[2 * LEN - 1:2 * LEN]
                for p in range(BLOCK // PART):
                    z_send[k * (BLOCK // PART) + p, r] = final[:, p * PART:(p + 1) * PART]
            return 0

        lax.fori_loop(0, REQ // 4, prefill, 0)
        if k == 0:
            pl.semaphore_wait(barrier, 2 + (GROUPS - 1) + (TENSORS - 1))
        for p in range(BLOCK // PART):
            j = k * (BLOCK // PART) + p
            copy = pltpu.make_async_remote_copy(
                z_send.at[j], z_recv[j], z_sem.at[0, j], z_sem.at[1, j],
                device_id=(ahead, group, tensor), device_id_type=MESH,
            )
            copy.start()
            z_out.append(copy)

    z_copy.wait()

    def gate(r, _):
        value = mixed[r] * silu(z_v[r].astype(F32))
        mixed[r] = value
        acc = jnp.zeros((LEN, 128), F32)
        for p in range(WIDTH // 128):
            part = value[:, p * 128:(p + 1) * 128]
            acc = acc + part * part
        squares[pl.ds(pl.multiple_of(r * LEN, LEN), LEN), :] = acc
        return 0

    lax.fori_loop(0, REQ, gate, 0)

    def exchange(which):
        copies = []
        for d in range(1, TENSORS):
            copy = pltpu.make_async_remote_copy(
                pack.at[which], got.at[which, d], t_sem.at[2 * which, d], t_sem.at[2 * which + 1, d],
                device_id=(section, group, lax.rem(tensor + d, TENSORS)), device_id_type=MESH,
            )
            copy.start()
            copies.append(copy)
        return copies

    pack[...] = jnp.zeros_like(pack)
    row8 = iota((8, 128), 0)
    packed = jnp.zeros((8, 128), F32)
    for q in range(4):
        sums = jnp.sum(jnp.transpose(squares[q * 128:(q + 1) * 128, :]), axis=0, keepdims=True)
        packed = jnp.where(row8 == q, sums, packed)
    pack[0] = packed
    pre_copies = exchange(0)

    turn[...] = jnp.zeros_like(turn)
    for s in range(REQ):
        turn[s * STEPS:(s + 1) * STEPS, 0:HEADS] = dec_dt[s]
    lane_d = iota((1, 128), 1)
    dec_step = softplus(turn[0:REQ * STEPS, :] + from_scalars(bias, lane_d, HEADS))
    dec_dec = jnp.exp(-from_scalars(rate, lane_d, HEADS) * dec_step)
    both = jnp.concatenate([dec_step, dec_dec], axis=0)
    heads_wide = (iota((128, WIDTH), 0) == iota((128, WIDTH), 1) // 64).astype(F32).astype(BF16)
    wide = sum(dot(term, heads_wide) for term in three_terms(both))
    pairs = REQ // 2
    dec_inject[...] = wide[0:REQ * STEPS].reshape(pairs, 8, WIDTH)
    dec_decay[...] = wide[REQ * STEPS:2 * REQ * STEPS].reshape(pairs, 8, WIDTH)
    skip_wide = from_scalars(skip, iota((1, WIDTH), 1) // 64, HEADS)
    for s in range(REQ):
        at = slice((s % 2) * STEPS, (s % 2) * STEPS + STEPS)
        x_f = dec_x[s].astype(F32)
        dec_inject[s // 2, at, :] = dec_inject[s // 2, at, :] * x_f
        dec_skip[s // 2, at, :] = skip_wide * x_f
        dec_gate[s // 2, at, :] = silu(dec_z[s].astype(F32))
    turn[...] = jnp.zeros_like(turn)
    for s in range(REQ):
        turn[s * STEPS:(s + 1) * STEPS, 0:STATE] = dec_b[s].astype(F32)
        turn[s * STEPS:(s + 1) * STEPS, STATE:2 * STATE] = dec_c[s].astype(F32)
    cols_t = jnp.transpose(turn[0:128, :])[0:2 * STATE]
    pick = (lax.rem(iota((128, WIDTH), 0), 8) == iota((128, WIDTH), 1) // 128).astype(F32).astype(BF16)
    lane_p = iota((2 * STATE, 128), 1) // 8

    for p in range(pairs):
        dec_cols[p] = dot(jnp.where(lane_p == p, cols_t, 0.0).astype(BF16), pick)
    dec_squares[...] = jnp.zeros_like(dec_squares)

    first_request = (behind * GROUPS + group) * REQ

    def find_source(h, _):
        low, high = jnp.int32(REQ - 1), jnp.int32(0)
        for r in range(REQ):
            is_it = owner[first_request + r] == h
            low = jnp.minimum(low, jnp.where(is_it, r, REQ - 1))
            high = jnp.maximum(high, jnp.where(is_it, r, 0))
        source[2 * h] = low
        source[2 * h + 1] = high
        return 0

    lax.fori_loop(0, GROUPS, find_source, 0)

    def find_rows(cell, carry):
        place, found = carry[0], carry[1:]
        count = jnp.int32(0)
        for r in range(REQ):
            count = count + jnp.where(owner[(behind * GROUPS + cell) * REQ + r] == group, 1, 0)
        has = jnp.where(count > 0, 1, 0)
        spot = jnp.where(count > 0, place, -1)
        return (place + has,) + tuple(jnp.where(spot == j, cell, v) for j, v in enumerate(found))

    found = lax.fori_loop(0, GROUPS, find_rows, (jnp.int32(0),) * (1 + REQ // 2))[1:]
    for j, cell in enumerate(found):
        rows[2 * j] = 2 * cell
        rows[2 * j + 1] = 2 * cell + 1

    def group_copy(j, d, count=1):
        rows_of = 2 * count
        return pltpu.make_async_remote_copy(
            x_send.at[j, pl.ds(2 * d, rows_of)],
            x_recv[j].at[pl.ds(2 * group if count == 1 else 2 * d, rows_of)],
            x_sem.at[0, j], x_sem.at[1, j],
            device_id=(section, group_at(d), tensor), device_id_type=MESH,
        )

    def forward(j):
        z_out[j].wait_recv()

        for p in range(2):
            x_recv[j][2 * group + p] = z_recv[j][source[2 * group + p]]

        def fill(d, _):
            h = group_at(d)
            for p in range(2):
                x_send[j, 2 * d + p] = z_recv[j][source[2 * h + p]]
            group_copy(j, d).start()
            return 0

        lax.fori_loop(1, GROUPS, fill, 0)

    state_out = []

    def decode(j):
        group_copy(j, 1, GROUPS - 1).wait_recv()
        cols = slice(j * PART, (j + 1) * PART)

        def pair(p, _):
            y = jnp.zeros((8, PART), F32)
            for i in range(2):
                state = x_recv[j][rows[2 * p + i]]
                for t in range(STEPS):
                    q = i * STEPS + t
                    b_col = dec_cols[p, 0:STATE, q * 128:(q + 1) * 128]
                    c_col = dec_cols[p, STATE:2 * STATE, q * 128:(q + 1) * 128]
                    state = state * dec_decay[p, q:q + 1, cols] + b_col * dec_inject[p, q:q + 1, cols]
                    y = jnp.where(row8 == q, jnp.sum(state * c_col, axis=0, keepdims=True), y)
                staged[2 * p + i, :, cols] = state
            value = (y + dec_skip[p, :, cols]) * dec_gate[p, :, cols]
            dec_gated[p, :, cols] = value
            at = pl.ds(pl.multiple_of(p * 8, 8), 8)
            dec_squares[at, :] = dec_squares[at, :] + value * value
            return 0

        lax.fori_loop(0, pairs, pair, 0)
        copy = pltpu.make_async_copy(
            staged.at[:, :, pl.ds(j * PART, PART)], state_hbm.at[:, :, pl.ds(j * PART, PART)],
            local_sem.at[blocks + 1 + j],
        )
        copy.start()
        state_out.append(copy)

    def summed(which, copies):
        for copy in copies:
            copy.wait_recv()
        acc = pack[which]
        for d in range(1, TENSORS):
            acc = acc + got[which, d]
        return lax.rsqrt(acc / CHAN + EPS)

    gain_row = gain[...]
    behind_by = 2
    pre_out = []
    for j in range(PARTS):
        forward(j)
        if j >= behind_by:
            decode(j - behind_by)
        if j == 3:
            scale = summed(0, pre_copies)
            lane_t = iota((8, 128), 1)
            req8 = row8 * 4 + lane_t // LEN
            scale = jnp.where(lax.rem(lane_t, LEN) < from_scalars(lengths, req8, REQ), scale, 0.0)
            for q in range(4):
                squares[q * 128:(q + 1) * 128, :] = jnp.transpose(
                    jnp.broadcast_to(scale[q:q + 1, :], (128, 128))
                )

            def finish(r, _):
                col = squares[pl.ds(pl.multiple_of(r * LEN, LEN), LEN), :]
                for p in range(WIDTH // 128):
                    at = slice(p * 128, (p + 1) * 128)
                    pre_v[r, :, at] = (mixed[r, :, at] * col * gain_row[:, at]).astype(BF16)
                return 0

            lax.fori_loop(0, REQ, finish, 0)
            copy = pltpu.make_async_copy(pre_v, pre_hbm, local_sem.at[blocks + 1 + PARTS])
            copy.start()
            pre_out.append(copy)
    for j in range(PARTS - behind_by, PARTS):
        decode(j)

    sums = jnp.sum(jnp.transpose(dec_squares[...]), axis=0, keepdims=True)
    pack[1] = jnp.broadcast_to(sums, (8, 128))
    dec_copies = exchange(1)
    scale = summed(1, dec_copies)
    column = jnp.transpose(jnp.broadcast_to(scale[0:1, :], (128, 128)))
    for p in range(pairs):
        col = column[p * 8:(p + 1) * 8, :]
        for c in range(WIDTH // 128):
            at = slice(c * 128, (c + 1) * 128)
            value = (dec_gated[p, :, at] * col * gain_row[:, at]).astype(BF16)
            dec_v[2 * p, :, at] = value[0:STEPS]
            dec_v[2 * p + 1, :, at] = value[STEPS:2 * STEPS]
    dec_copy = pltpu.make_async_copy(dec_v, dec_hbm, local_sem.at[blocks + 2 + PARTS])
    dec_copy.start()

    for j in range(PARTS):
        z_out[j].wait_send()
        group_copy(j, 1, GROUPS - 1).wait_send()
    for copy in pre_copies + dec_copies:
        copy.wait_send()
    for copy in state_out + pre_out:
        copy.wait()
    dec_copy.wait()


def local(
    x_pre, z_pre, b_pre, c_pre, dt_pre, lengths, owner,
    dec_x, dec_z, dec_b, dec_c, dec_dt, decay_rate, dt_bias, skip, norm_gain,
):
    smem = pl.BlockSpec(memory_space=pltpu.SMEM)
    vmem = pl.BlockSpec(memory_space=pltpu.VMEM)
    anywhere = pl.BlockSpec(memory_space=pl.ANY)
    tokens = (REQ, LEN, WIDTH)
    steps = (REQ // 2, 8, WIDTH)
    scratch = [
        pltpu.VMEM(tokens, BF16),
        pltpu.VMEM(tokens, BF16),
        pltpu.VMEM((REQ * HEADS, 128), F32),
        pltpu.VMEM((REQ, LEN + STATE, 3 * LEN), BF16),
        pltpu.VMEM((REQ, 2 * LEN, 256), BF16),
        pltpu.VMEM(tokens, F32),
        pltpu.VMEM((REQ * LEN, 128), F32),
        pltpu.VMEM((PARTS, REQ, STATE, PART), F32),
        pltpu.VMEM((PARTS, 2 * GROUPS, STATE, PART), F32),
        pltpu.VMEM((REQ, STATE, WIDTH), F32),
        pltpu.VMEM(tokens, BF16),
        pltpu.VMEM((REQ, STEPS, WIDTH), BF16),
        pltpu.VMEM(steps, F32),
        pltpu.VMEM(steps, F32),
        pltpu.VMEM(steps, F32),
        pltpu.VMEM(steps, F32),
        pltpu.VMEM((REQ // 2, 2 * STATE, WIDTH), F32),
        pltpu.VMEM(steps, F32),
        pltpu.VMEM((128, 128), F32),
        pltpu.VMEM((2, 8, 128), F32),
        pltpu.VMEM((2, TENSORS, 8, 128), F32),
        pltpu.SMEM((2 * GROUPS,), jnp.int32),
        pltpu.SMEM((REQ,), jnp.int32),
        pltpu.SemaphoreType.DMA((WIDTH // BLOCK + 3 + PARTS,)),
        pltpu.SemaphoreType.DMA((2, PARTS)),
        pltpu.SemaphoreType.DMA((2, PARTS)),
        pltpu.SemaphoreType.DMA((4, TENSORS)),
    ]
    scratch += [pltpu.VMEM((REQ, STATE, PART), F32) for _ in range(PARTS)]
    scratch += [pltpu.VMEM((2 * GROUPS, STATE, PART), F32) for _ in range(PARTS)]
    return pl.pallas_call(
        kernel,
        out_shape=(
            jax.ShapeDtypeStruct(tokens, BF16),
            jax.ShapeDtypeStruct((REQ, STEPS, WIDTH), BF16),
            jax.ShapeDtypeStruct((REQ, STATE, WIDTH), F32),
        ),
        in_specs=[smem] * 5 + [vmem] * 9 + [anywhere] * 2,
        out_specs=(anywhere, anywhere, anywhere),
        scratch_shapes=scratch,
        compiler_params=pltpu.CompilerParams(
            collective_id=0, has_side_effects=True, vmem_limit_bytes=56 << 20
        ),
    )(
        lengths, owner, decay_rate, dt_bias, skip,
        jnp.transpose(b_pre, (0, 2, 1)), jnp.transpose(c_pre, (0, 2, 1)), jnp.transpose(dt_pre, (0, 2, 1)),
        dec_x, dec_z, dec_b, dec_c, dec_dt, norm_gain.reshape(1, WIDTH),
        x_pre, z_pre,
    )


def solution(mesh):
    cell = ("section", "group")
    return jax.shard_map(
        local,
        mesh=mesh,
        in_specs=(
            P(cell, None, "tensor"), P(cell, None, "tensor"), P(cell, None, None), P(cell, None, None),
            P(cell, None, "tensor"), P(cell), P(), P(cell, None, "tensor"), P(cell, None, "tensor"),
            P(cell, None, None), P(cell, None, None), P(cell, None, "tensor"),
            P("tensor"), P("tensor"), P("tensor"), P("tensor"),
        ),
        out_specs=(P(cell, None, "tensor"),) * 3,
        check_vma=False,
    )
```

```python
import functools

import jax
import jax.numpy as jnp
from jax import lax
from jax.experimental import pallas as pl
from jax.experimental.pallas import tpu as pltpu
from jax.sharding import PartitionSpec as P

CHAN = 8192
EPS = 1e-05
MESH = pl.DeviceIdType.MESH
F32 = jnp.float32
BF16 = jnp.bfloat16

REQ = 16
LEN = 32
STATE = 16
HEADS = 16
WIDTH = 1024
STEPS = 4
SIDE = 4
GROUPS = 16
SECTIONS = 4
TENSORS = 8
PARTS = 8
PART = WIDTH // PARTS
BLOCK = 256
UNROLL = 8


def iota(shape, dim):
    return lax.broadcasted_iota(jnp.int32, shape, dim)


def softplus(v):
    return jnp.maximum(v, 0.0) + jnp.log1p(jnp.exp(-jnp.abs(v)))


def silu(v):
    return v / (1.0 + jnp.exp(-v))


def two_terms(v):
    high = v.astype(BF16)
    return high, (v - high.astype(F32)).astype(BF16)


def three_terms(v):
    high = v.astype(BF16)
    rest = v - high.astype(F32)
    mid = rest.astype(BF16)
    return high, mid, (rest - mid.astype(F32)).astype(BF16)


def dot(a, b):
    return jnp.dot(a, b, preferred_element_type=F32)


def from_scalars(ref, where_index, count):
    acc = jnp.zeros(where_index.shape, ref.dtype)
    for k in range(count):
        acc = jnp.where(where_index == k, ref[k], acc)
    return acc


def kernel(
    lengths, owner, rate, bias, skip,
    b_t, c_t, dt_t, dec_x, dec_z, dec_b, dec_c, dec_dt, gain,
    x_hbm, z_hbm,
    pre_hbm, dec_hbm, state_hbm,
    *scratch,
):
    (x_v, z_v, turn, lhs, expand_lhs, mixed, squares, z_send, x_send, staged, pre_v,
     dec_v, dec_decay, dec_inject, dec_skip, dec_gate, dec_cols, dec_gated, dec_squares,
     pack, got, source, rows, local_sem, z_sem, x_sem, t_sem) = scratch[:27]
    z_recv = scratch[27:27 + PARTS]
    x_recv = scratch[27 + PARTS:27 + 2 * PARTS]

    section = lax.axis_index("section")
    group = lax.axis_index("group")
    tensor = lax.axis_index("tensor")
    gx, gy = group // SIDE, lax.rem(group, SIDE)
    ahead = lax.rem(section + 1, SECTIONS)
    behind = lax.rem(section + SECTIONS - 1, SECTIONS)

    def group_at(d):
        return lax.rem(gx + d // SIDE, SIDE) * SIDE + lax.rem(gy + lax.rem(d, SIDE), SIDE)

    blocks = WIDTH // BLOCK
    x_copies = []
    for k in range(blocks):
        cols = pl.ds(k * BLOCK, BLOCK)
        copy = pltpu.make_async_copy(x_hbm.at[:, :, cols], x_v.at[:, :, cols], local_sem.at[k])
        copy.start()
        x_copies.append(copy)
    z_copy = pltpu.make_async_copy(z_hbm, z_v, local_sem.at[blocks])
    z_copy.start()

    barrier = pltpu.get_barrier_semaphore()
    for to in (ahead, behind):
        pl.semaphore_signal(barrier, inc=1, device_id=(to, group, tensor), device_id_type=MESH)
    for d in range(1, GROUPS):
        pl.semaphore_signal(barrier, inc=1, device_id=(section, group_at(d), tensor), device_id_type=MESH)
    for d in range(1, TENSORS):
        pl.semaphore_signal(
            barrier, inc=1, device_id=(section, group, lax.rem(tensor + d, TENSORS)), device_id_type=MESH
        )

    turn[...] = jnp.zeros_like(turn)
    turn[:, 0:LEN] = dt_t[...].reshape(REQ * HEADS, LEN)
    logits = jnp.transpose(turn[...])[0:LEN]
    lane = iota((1, REQ * HEADS), 1)
    head_of, req_of = lax.rem(lane, HEADS), lane // HEADS
    live = iota((LEN, REQ * HEADS), 0) < from_scalars(lengths, req_of, REQ)
    step = jnp.where(live, softplus(logits + from_scalars(bias, head_of, HEADS)), 0.0)
    fall = from_scalars(rate, head_of, HEADS) * step
    lower = (iota((LEN, LEN), 0) >= iota((LEN, LEN), 1)).astype(F32).astype(BF16)
    total = sum(dot(lower, term) for term in three_terms(fall))
    shrink = jnp.exp(-total)
    grow = jnp.exp(total) * step

    turn[:, 0:LEN] = c_t[...].reshape(REQ * STATE, LEN).astype(F32)
    c_tok = jnp.transpose(turn[...])[0:LEN]
    spread = (lax.rem(iota((LEN, 3 * LEN), 1), LEN) == iota((LEN, 3 * LEN), 0)).astype(F32).astype(BF16)
    b_rep = dot(b_t[...].reshape(REQ * STATE, LEN), spread)
    lane3 = iota((LEN, 3 * LEN), 1)
    middle = (lane3 >= LEN) & (lane3 < 2 * LEN)
    causal = iota((LEN, 3 * LEN), 0) >= lax.rem(lane3, LEN)
    lane128 = iota((LEN, 128), 1) // HEADS
    half_reqs = 128 // HEADS
    for r in range(REQ):
        half = slice((r // half_reqs) * 128, (r // half_reqs) * 128 + 128)
        mine = lane128 == r % half_reqs
        for at, values in ((0, grow), (LEN, shrink)):
            high, low = two_terms(values[:, r * HEADS:(r + 1) * HEADS])
            expand_lhs[r, at:at + LEN, 0:HEADS] = high
            expand_lhs[r, at:at + LEN, HEADS:2 * HEADS] = low
        gram = dot(jnp.where(mine, c_tok[:, half], 0.0).astype(BF16), b_rep[half].astype(BF16))
        high = gram.astype(BF16).astype(F32)
        lhs[r, 0:LEN, :] = jnp.where(causal, jnp.where(middle, gram - high, high), 0.0).astype(BF16)
        lhs[r, LEN:LEN + STATE, :] = jnp.where(
            middle[0:STATE], 0.0, b_rep[r * STATE:(r + 1) * STATE]
        ).astype(BF16)

    z_out = []

    def states(k):
        x_copies[k].wait()
        cols = slice(k * BLOCK, (k + 1) * BLOCK)
        head_rows = lax.rem(iota((2 * HEADS, BLOCK), 0), HEADS)
        head_cols = iota((2 * HEADS, BLOCK), 1) // 64 + k * (BLOCK // 64)
        expand = (head_rows == head_cols).astype(F32).astype(BF16)
        skip_row = from_scalars(skip, iota((1, BLOCK), 1) // 64 + k * (BLOCK // 64), HEADS)

        def prefill(i, _):
            first = i * UNROLL
            wides = dot(expand_lhs[pl.ds(first, UNROLL)].reshape(UNROLL * 2 * LEN, 2 * HEADS), expand)
            for sub in range(UNROLL):
                r = first + sub
                wide = wides[sub * 2 * LEN:(sub + 1) * 2 * LEN]
                x_f = x_v[r, :, cols].astype(F32)
                high, low = two_terms(x_f * wide[0:LEN])
                res = dot(lhs[r], jnp.concatenate([high, high, low], axis=0))
                mixed[r, :, cols] = res[0:LEN] * wide[LEN:2 * LEN] + skip_row * x_f
                final = res[LEN:LEN + STATE] * wide[2 * LEN - 1:2 * LEN]
                for p in range(BLOCK // PART):
                    z_send[k * (BLOCK // PART) + p, r] = final[:, p * PART:(p + 1) * PART]
            return 0

        lax.fori_loop(0, REQ // UNROLL, prefill, 0)

    def send_on(k):
        for p in range(BLOCK // PART):
            j = k * (BLOCK // PART) + p
            copy = pltpu.make_async_remote_copy(
                z_send.at[j], z_recv[j], z_sem.at[0, j], z_sem.at[1, j],
                device_id=(ahead, group, tensor), device_id_type=MESH,
            )
            copy.start()
            z_out.append(copy)

    states(0)
    pl.semaphore_wait(barrier, 2 + (GROUPS - 1) + (TENSORS - 1))
    send_on(0)
    states(1)
    send_on(1)

    first_request = (behind * GROUPS + group) * REQ

    def find_source(h, _):
        low, high = jnp.int32(REQ - 1), jnp.int32(0)
        for r in range(REQ):
            is_it = owner[first_request + r] == h
            low = jnp.minimum(low, jnp.where(is_it, r, REQ - 1))
            high = jnp.maximum(high, jnp.where(is_it, r, 0))
        source[2 * h] = low
        source[2 * h + 1] = high
        return 0

    lax.fori_loop(0, GROUPS, find_source, 0)

    def find_rows(cell, carry):
        place, found = carry[0], carry[1:]
        count = jnp.int32(0)
        for r in range(REQ):
            count = count + jnp.where(owner[(behind * GROUPS + cell) * REQ + r] == group, 1, 0)
        has = jnp.where(count > 0, 1, 0)
        spot = jnp.where(count > 0, place, -1)
        return (place + has,) + tuple(jnp.where(spot == j, cell, v) for j, v in enumerate(found))

    found = lax.fori_loop(0, GROUPS, find_rows, (jnp.int32(0),) * (1 + REQ // 2))[1:]
    for j, cell in enumerate(found):
        rows[2 * j] = 2 * cell
        rows[2 * j + 1] = 2 * cell + 1

    def group_copy(j, d, count=1):
        rows_of = 2 * count
        return pltpu.make_async_remote_copy(
            x_send.at[j, pl.ds(2 * d, rows_of)],
            x_recv[j].at[pl.ds(2 * group if count == 1 else 2 * d, rows_of)],
            x_sem.at[0, j], x_sem.at[1, j],
            device_id=(section, group_at(d), tensor), device_id_type=MESH,
        )

    def forward(j):
        z_out[j].wait_recv()

        for p in range(2):
            x_recv[j][2 * group + p] = z_recv[j][source[2 * group + p]]

        def fill(d, _):
            h = group_at(d)
            for p in range(2):
                x_send[j, 2 * d + p] = z_recv[j][source[2 * h + p]]
            group_copy(j, d).start()
            return 0

        lax.fori_loop(1, GROUPS, fill, 0)

    forward(0)
    states(2)
    send_on(2)
    forward(1)
    states(3)
    send_on(3)
    forward(2)

    z_copy.wait()

    def gate(r, _):
        value = mixed[r] * silu(z_v[r].astype(F32))
        mixed[r] = value
        acc = jnp.zeros((LEN, 128), F32)
        for p in range(WIDTH // 128):
            part = value[:, p * 128:(p + 1) * 128]
            acc = acc + part * part
        squares[pl.ds(pl.multiple_of(r * LEN, LEN), LEN), :] = acc
        return 0

    lax.fori_loop(0, REQ, gate, 0)

    def exchange(which):
        copies = []
        for d in range(1, TENSORS):
            copy = pltpu.make_async_remote_copy(
                pack.at[which], got.at[which, d], t_sem.at[2 * which, d], t_sem.at[2 * which + 1, d],
                device_id=(section, group, lax.rem(tensor + d, TENSORS)), device_id_type=MESH,
            )
            copy.start()
            copies.append(copy)
        return copies

    pack[...] = jnp.zeros_like(pack)
    row8 = iota((8, 128), 0)
    packed = jnp.zeros((8, 128), F32)
    for q in range(4):
        sums = jnp.sum(jnp.transpose(squares[q * 128:(q + 1) * 128, :]), axis=0, keepdims=True)
        packed = jnp.where(row8 == q, sums, packed)
    pack[0] = packed
    pre_copies = exchange(0)

    turn[...] = jnp.zeros_like(turn)
    for s in range(REQ):
        turn[s * STEPS:(s + 1) * STEPS, 0:HEADS] = dec_dt[s]
    lane_d = iota((1, 128), 1)
    dec_step = softplus(turn[0:REQ * STEPS, :] + from_scalars(bias, lane_d, HEADS))
    dec_dec = jnp.exp(-from_scalars(rate, lane_d, HEADS) * dec_step)
    both = jnp.concatenate([dec_step, dec_dec], axis=0)
    heads_wide = (iota((128, WIDTH), 0) == iota((128, WIDTH), 1) // 64).astype(F32).astype(BF16)
    wide = sum(dot(term, heads_wide) for term in three_terms(both))
    pairs = REQ // 2
    dec_inject[...] = wide[0:REQ * STEPS].reshape(pairs, 8, WIDTH)
    dec_decay[...] = wide[REQ * STEPS:2 * REQ * STEPS].reshape(pairs, 8, WIDTH)
    skip_wide = from_scalars(skip, iota((1, WIDTH), 1) // 64, HEADS)
    for s in range(REQ):
        at = slice((s % 2) * STEPS, (s % 2) * STEPS + STEPS)
        x_f = dec_x[s].astype(F32)
        dec_inject[s // 2, at, :] = dec_inject[s // 2, at, :] * x_f
        dec_skip[s // 2, at, :] = skip_wide * x_f
        dec_gate[s // 2, at, :] = silu(dec_z[s].astype(F32))
    turn[...] = jnp.zeros_like(turn)
    for s in range(REQ):
        turn[s * STEPS:(s + 1) * STEPS, 0:STATE] = dec_b[s].astype(F32)
        turn[s * STEPS:(s + 1) * STEPS, STATE:2 * STATE] = dec_c[s].astype(F32)
    cols_t = jnp.transpose(turn[0:128, :])[0:2 * STATE]
    pick = (lax.rem(iota((128, WIDTH), 0), 8) == iota((128, WIDTH), 1) // 128).astype(F32).astype(BF16)
    lane_p = iota((2 * STATE, 128), 1) // 8

    for p in range(pairs):
        dec_cols[p] = dot(jnp.where(lane_p == p, cols_t, 0.0).astype(BF16), pick)
    dec_squares[...] = jnp.zeros_like(dec_squares)

    state_out = []

    def decode(j):
        group_copy(j, 1, GROUPS - 1).wait_recv()
        cols = slice(j * PART, (j + 1) * PART)

        def pair(p, _):
            y = jnp.zeros((8, PART), F32)
            for i in range(2):
                state = x_recv[j][rows[2 * p + i]]
                for t in range(STEPS):
                    q = i * STEPS + t
                    b_col = dec_cols[p, 0:STATE, q * 128:(q + 1) * 128]
                    c_col = dec_cols[p, STATE:2 * STATE, q * 128:(q + 1) * 128]
                    state = state * dec_decay[p, q:q + 1, cols] + b_col * dec_inject[p, q:q + 1, cols]
                    y = jnp.where(row8 == q, jnp.sum(state * c_col, axis=0, keepdims=True), y)
                staged[2 * p + i, :, cols] = state
            value = (y + dec_skip[p, :, cols]) * dec_gate[p, :, cols]
            dec_gated[p, :, cols] = value
            at = pl.ds(pl.multiple_of(p * 8, 8), 8)
            dec_squares[at, :] = dec_squares[at, :] + value * value
            return 0

        lax.fori_loop(0, pairs, pair, 0)
        copy = pltpu.make_async_copy(
            staged.at[:, :, pl.ds(j * PART, PART)], state_hbm.at[:, :, pl.ds(j * PART, PART)],
            local_sem.at[blocks + 1 + j],
        )
        copy.start()
        state_out.append(copy)

    def summed(which, copies):
        for copy in copies:
            copy.wait_recv()
        acc = pack[which]
        for d in range(1, TENSORS):
            acc = acc + got[which, d]
        return lax.rsqrt(acc / CHAN + EPS)

    gain_row = gain[...]
    pre_out = []
    for j in range(3, PARTS):
        forward(j)
        decode(j - 3)
    scale = summed(0, pre_copies)
    lane_t = iota((8, 128), 1)
    req8 = row8 * 4 + lane_t // LEN
    scale = jnp.where(lax.rem(lane_t, LEN) < from_scalars(lengths, req8, REQ), scale, 0.0)
    for q in range(4):
        squares[q * 128:(q + 1) * 128, :] = jnp.transpose(
            jnp.broadcast_to(scale[q:q + 1, :], (128, 128))
        )

    def finish(r, _):
        col = squares[pl.ds(pl.multiple_of(r * LEN, LEN), LEN), :]
        for p in range(WIDTH // 128):
            at = slice(p * 128, (p + 1) * 128)
            pre_v[r, :, at] = (mixed[r, :, at] * col * gain_row[:, at]).astype(BF16)
        return 0

    lax.fori_loop(0, REQ, finish, 0)
    copy = pltpu.make_async_copy(pre_v, pre_hbm, local_sem.at[blocks + 1 + PARTS])
    copy.start()
    pre_out.append(copy)
    for j in range(PARTS - 3, PARTS):
        decode(j)

    sums = jnp.sum(jnp.transpose(dec_squares[...]), axis=0, keepdims=True)
    pack[1] = jnp.broadcast_to(sums, (8, 128))
    dec_copies = exchange(1)
    scale = summed(1, dec_copies)
    column = jnp.transpose(jnp.broadcast_to(scale[0:1, :], (128, 128)))
    for p in range(pairs):
        col = column[p * 8:(p + 1) * 8, :]
        for c in range(WIDTH // 128):
            at = slice(c * 128, (c + 1) * 128)
            value = (dec_gated[p, :, at] * col * gain_row[:, at]).astype(BF16)
            dec_v[2 * p, :, at] = value[0:STEPS]
            dec_v[2 * p + 1, :, at] = value[STEPS:2 * STEPS]
    dec_copy = pltpu.make_async_copy(dec_v, dec_hbm, local_sem.at[blocks + 2 + PARTS])
    dec_copy.start()

    for j in range(PARTS):
        z_out[j].wait_send()
        group_copy(j, 1, GROUPS - 1).wait_send()
    for copy in pre_copies + dec_copies:
        copy.wait_send()
    for copy in state_out + pre_out:
        copy.wait()
    dec_copy.wait()


def local(
    x_pre, z_pre, b_pre, c_pre, dt_pre, lengths, owner,
    dec_x, dec_z, dec_b, dec_c, dec_dt, decay_rate, dt_bias, skip, norm_gain,
):
    smem = pl.BlockSpec(memory_space=pltpu.SMEM)
    vmem = pl.BlockSpec(memory_space=pltpu.VMEM)
    anywhere = pl.BlockSpec(memory_space=pl.ANY)
    tokens = (REQ, LEN, WIDTH)
    steps = (REQ // 2, 8, WIDTH)
    scratch = [
        pltpu.VMEM(tokens, BF16),
        pltpu.VMEM(tokens, BF16),
        pltpu.VMEM((REQ * HEADS, 128), F32),
        pltpu.VMEM((REQ, LEN + STATE, 3 * LEN), BF16),
        pltpu.VMEM((REQ, 2 * LEN, 2 * HEADS), BF16),
        pltpu.VMEM(tokens, F32),
        pltpu.VMEM((REQ * LEN, 128), F32),
        pltpu.VMEM((PARTS, REQ, STATE, PART), F32),
        pltpu.VMEM((PARTS, 2 * GROUPS, STATE, PART), F32),
        pltpu.VMEM((REQ, STATE, WIDTH), F32),
        pltpu.VMEM(tokens, BF16),
        pltpu.VMEM((REQ, STEPS, WIDTH), BF16),
        pltpu.VMEM(steps, F32),
        pltpu.VMEM(steps, F32),
        pltpu.VMEM(steps, F32),
        pltpu.VMEM(steps, F32),
        pltpu.VMEM((REQ // 2, 2 * STATE, WIDTH), F32),
        pltpu.VMEM(steps, F32),
        pltpu.VMEM((128, 128), F32),
        pltpu.VMEM((2, 8, 128), F32),
        pltpu.VMEM((2, TENSORS, 8, 128), F32),
        pltpu.SMEM((2 * GROUPS,), jnp.int32),
        pltpu.SMEM((REQ,), jnp.int32),
        pltpu.SemaphoreType.DMA((WIDTH // BLOCK + 3 + PARTS,)),
        pltpu.SemaphoreType.DMA((2, PARTS)),
        pltpu.SemaphoreType.DMA((2, PARTS)),
        pltpu.SemaphoreType.DMA((4, TENSORS)),
    ]
    scratch += [pltpu.VMEM((REQ, STATE, PART), F32) for _ in range(PARTS)]
    scratch += [pltpu.VMEM((2 * GROUPS, STATE, PART), F32) for _ in range(PARTS)]
    return pl.pallas_call(
        kernel,
        out_shape=(
            jax.ShapeDtypeStruct(tokens, BF16),
            jax.ShapeDtypeStruct((REQ, STEPS, WIDTH), BF16),
            jax.ShapeDtypeStruct((REQ, STATE, WIDTH), F32),
        ),
        in_specs=[smem] * 5 + [vmem] * 9 + [anywhere] * 2,
        out_specs=(anywhere, anywhere, anywhere),
        scratch_shapes=scratch,
        compiler_params=pltpu.CompilerParams(
            collective_id=0, has_side_effects=True, vmem_limit_bytes=56 << 20
        ),
    )(
        lengths, owner, decay_rate, dt_bias, skip,
        jnp.transpose(b_pre, (0, 2, 1)), jnp.transpose(c_pre, (0, 2, 1)), jnp.transpose(dt_pre, (0, 2, 1)),
        dec_x, dec_z, dec_b, dec_c, dec_dt, norm_gain.reshape(1, WIDTH),
        x_pre, z_pre,
    )


def solution(mesh):
    cell = ("section", "group")
    return jax.shard_map(
        local,
        mesh=mesh,
        in_specs=(
            P(cell, None, "tensor"), P(cell, None, "tensor"), P(cell, None, None), P(cell, None, None),
            P(cell, None, "tensor"), P(cell), P(), P(cell, None, "tensor"), P(cell, None, "tensor"),
            P(cell, None, None), P(cell, None, None), P(cell, None, "tensor"),
            P("tensor"), P("tensor"), P("tensor"), P("tensor"),
        ),
        out_specs=(P(cell, None, "tensor"),) * 3,
        check_vma=False,
    )
```

```python
import functools

import jax
import jax.numpy as jnp
from jax import lax
from jax.experimental import pallas as pl
from jax.experimental.pallas import tpu as pltpu
from jax.sharding import PartitionSpec as P

CHAN = 8192
EPS = 1e-05
MESH = pl.DeviceIdType.MESH
F32 = jnp.float32
BF16 = jnp.bfloat16

REQ = 16
LEN = 32
STATE = 16
HEADS = 16
WIDTH = 1024
STEPS = 4
SIDE = 4
GROUPS = 16
SECTIONS = 4
TENSORS = 8
PARTS = 8
PART = WIDTH // PARTS
BLOCK = 256
GROUP_FIRST = (0, 1, 4, 5)
PLACE_PARTS = 4
UNROLL = 8


def iota(shape, dim):
    return lax.broadcasted_iota(jnp.int32, shape, dim)


def softplus(v):
    return jnp.maximum(v, 0.0) + jnp.log1p(jnp.exp(-jnp.abs(v)))


def silu(v):
    return v / (1.0 + jnp.exp(-v))


def two_terms(v):
    high = v.astype(BF16)
    return high, (v - high.astype(F32)).astype(BF16)


def three_terms(v):
    high = v.astype(BF16)
    rest = v - high.astype(F32)
    mid = rest.astype(BF16)
    return high, mid, (rest - mid.astype(F32)).astype(BF16)


def dot(a, b):
    return jnp.dot(a, b, preferred_element_type=F32)


def from_scalars(ref, where_index, count):
    acc = jnp.zeros(where_index.shape, ref.dtype)
    for k in range(count):
        acc = jnp.where(where_index == k, ref[k], acc)
    return acc


def kernel(
    lengths, owner, rate, bias, skip,
    b_t, c_t, dt_t, dec_x, dec_z, dec_b, dec_c, dec_dt, gain,
    x_hbm, z_hbm,
    pre_hbm, dec_hbm, state_hbm,
    *scratch,
):
    (x_v, z_v, turn, lhs, expand_lhs, mixed, squares, z_send, x_send, staged, pre_v,
     dec_v, dec_decay, dec_inject, dec_skip, dec_gate, dec_cols, dec_gated, dec_squares,
     pack, got, source, rows, local_sem, z_sem, x_sem, t_sem, relay) = scratch[:28]
    z_recv = scratch[28:28 + PARTS]
    x_recv = scratch[28 + PARTS:28 + 2 * PARTS]

    section = lax.axis_index("section")
    group = lax.axis_index("group")
    tensor = lax.axis_index("tensor")
    gx, gy = group // SIDE, lax.rem(group, SIDE)
    ahead = lax.rem(section + 1, SECTIONS)
    behind = lax.rem(section + SECTIONS - 1, SECTIONS)

    def farther_first(a):
        return lax.rem(2 + a + a // 2 + 2 * (a // 3), SIDE)

    def group_at(d):
        by_x, by_y = farther_first(d // SIDE), farther_first(lax.rem(d, SIDE))
        return lax.rem(gx + by_x, SIDE) * SIDE + lax.rem(gy + by_y, SIDE)

    blocks = WIDTH // BLOCK
    x_copies = []
    for k in range(blocks):
        cols = pl.ds(k * BLOCK, BLOCK)
        copy = pltpu.make_async_copy(x_hbm.at[:, :, cols], x_v.at[:, :, cols], local_sem.at[k])
        copy.start()
        x_copies.append(copy)
    z_copy = pltpu.make_async_copy(z_hbm, z_v, local_sem.at[blocks])
    z_copy.start()

    barrier = pltpu.get_barrier_semaphore()
    for to in (ahead, behind):
        pl.semaphore_signal(barrier, inc=1, device_id=(to, group, tensor), device_id_type=MESH)
    for d in range(GROUPS - 1):
        pl.semaphore_signal(barrier, inc=1, device_id=(section, group_at(d), tensor), device_id_type=MESH)
    core = lax.rem(tensor, 2)
    near = [tensor + 1 - 2 * core]
    for by in (2, TENSORS - 2):
        near += [lax.rem(tensor - core + by, TENSORS) + c for c in range(2)]
    for to in near:
        pl.semaphore_signal(barrier, inc=1, device_id=(section, group, to), device_id_type=MESH)

    turn[...] = jnp.zeros_like(turn)
    turn[:, 0:LEN] = dt_t[...].reshape(REQ * HEADS, LEN)
    logits = jnp.transpose(turn[...])[0:LEN]
    lane = iota((1, REQ * HEADS), 1)
    head_of, req_of = lax.rem(lane, HEADS), lane // HEADS
    live = iota((LEN, REQ * HEADS), 0) < from_scalars(lengths, req_of, REQ)
    step = jnp.where(live, softplus(logits + from_scalars(bias, head_of, HEADS)), 0.0)
    fall = from_scalars(rate, head_of, HEADS) * step
    lower = (iota((LEN, LEN), 0) >= iota((LEN, LEN), 1)).astype(F32).astype(BF16)
    total = sum(dot(lower, term) for term in three_terms(fall))
    shrink = jnp.exp(-total)
    grow = jnp.exp(total) * step

    turn[:, 0:LEN] = c_t[...].reshape(REQ * STATE, LEN).astype(F32)
    c_tok = jnp.transpose(turn[...])[0:LEN]
    spread = (lax.rem(iota((LEN, 3 * LEN), 1), LEN) == iota((LEN, 3 * LEN), 0)).astype(F32).astype(BF16)
    b_rep = dot(b_t[...].reshape(REQ * STATE, LEN), spread)
    lane3 = iota((LEN, 3 * LEN), 1)
    middle = (lane3 >= LEN) & (lane3 < 2 * LEN)
    causal = iota((LEN, 3 * LEN), 0) >= lax.rem(lane3, LEN)
    lane128 = iota((LEN, 128), 1) // HEADS
    half_reqs = 128 // HEADS
    for r in range(REQ):
        half = slice((r // half_reqs) * 128, (r // half_reqs) * 128 + 128)
        mine = lane128 == r % half_reqs
        for at, values in ((0, grow), (LEN, shrink)):
            high, low = two_terms(values[:, r * HEADS:(r + 1) * HEADS])
            expand_lhs[r, at:at + LEN, 0:HEADS] = high
            expand_lhs[r, at:at + LEN, HEADS:2 * HEADS] = low
        gram = dot(jnp.where(mine, c_tok[:, half], 0.0).astype(BF16), b_rep[half].astype(BF16))
        high = gram.astype(BF16).astype(F32)
        lhs[r, 0:LEN, :] = jnp.where(causal, jnp.where(middle, gram - high, high), 0.0).astype(BF16)
        lhs[r, LEN:LEN + STATE, :] = jnp.where(
            middle[0:STATE], 0.0, b_rep[r * STATE:(r + 1) * STATE]
        ).astype(BF16)

    def states(k):
        x_copies[k].wait()
        cols = slice(k * BLOCK, (k + 1) * BLOCK)
        head_rows = lax.rem(iota((2 * HEADS, BLOCK), 0), HEADS)
        head_cols = iota((2 * HEADS, BLOCK), 1) // 64 + k * (BLOCK // 64)
        expand = (head_rows == head_cols).astype(F32).astype(BF16)
        skip_row = from_scalars(skip, iota((1, BLOCK), 1) // 64 + k * (BLOCK // 64), HEADS)

        def prefill(i, _):
            first = i * UNROLL
            wides = dot(expand_lhs[pl.ds(first, UNROLL)].reshape(UNROLL * 2 * LEN, 2 * HEADS), expand)
            for sub in range(UNROLL):
                r = first + sub
                wide = wides[sub * 2 * LEN:(sub + 1) * 2 * LEN]
                x_f = x_v[r, :, cols].astype(F32)
                high, low = two_terms(x_f * wide[0:LEN])
                res = dot(lhs[r], jnp.concatenate([high, high, low], axis=0))
                mixed[r, :, cols] = res[0:LEN] * wide[LEN:2 * LEN] + skip_row * x_f
                final = res[LEN:LEN + STATE] * wide[2 * LEN - 1:2 * LEN]
                for p in range(BLOCK // PART):
                    z_send[k * (BLOCK // PART) + p, r] = final[:, p * PART:(p + 1) * PART]
            return 0

        lax.fori_loop(0, REQ // UNROLL, prefill, 0)

    def section_copy(j):
        return pltpu.make_async_remote_copy(
            z_send.at[j], z_recv[j], z_sem.at[0, j], z_sem.at[1, j],
            device_id=(ahead, group, tensor), device_id_type=MESH,
        )

    def find(at, from_section):
        first_request = (from_section * GROUPS + group) * REQ

        def find_source(h, _):
            low, high = jnp.int32(REQ - 1), jnp.int32(0)
            for r in range(REQ):
                is_it = owner[first_request + r] == h
                low = jnp.minimum(low, jnp.where(is_it, r, REQ - 1))
                high = jnp.maximum(high, jnp.where(is_it, r, 0))
            source[at, 2 * h] = low
            source[at, 2 * h + 1] = high
            return 0

        def find_rows(cell, carry):
            place, found = carry[0], carry[1:]
            count = jnp.int32(0)
            for r in range(REQ):
                is_it = owner[(from_section * GROUPS + cell) * REQ + r] == group
                count = count + jnp.where(is_it, 1, 0)
            has = jnp.where(count > 0, 1, 0)
            spot = jnp.where(count > 0, place, -1)
            return (place + has,) + tuple(jnp.where(spot == j, cell, v) for j, v in enumerate(found))

        lax.fori_loop(0, GROUPS, find_source, 0)
        found = lax.fori_loop(0, GROUPS, find_rows, (jnp.int32(0),) * (1 + REQ // 2))[1:]
        for j, cell in enumerate(found):
            rows[at, 2 * j] = 2 * cell
            rows[at, 2 * j + 1] = 2 * cell + 1

    def group_copy(j, d, count=1):
        rows_of = 2 * count
        return pltpu.make_async_remote_copy(
            x_send.at[j, pl.ds(2 * d, rows_of)],
            x_recv[j].at[pl.ds(2 * group if count == 1 else 2 * d, rows_of)],
            x_sem.at[0, j], x_sem.at[1, j],
            device_id=(section, group_at(d), tensor), device_id_type=MESH,
        )

    def to_groups(j, state_of, at):
        for p in range(2):
            x_recv[j][2 * group + p] = state_of(source[at, 2 * group + p])

        def fill(d, _):
            h = group_at(d)
            for p in range(2):
                x_send[j, 2 * d + p] = state_of(source[at, 2 * h + p])
            group_copy(j, d).start()
            return 0

        lax.fori_loop(0, GROUPS - 1, fill, 0)

    def group_second(j):
        section_copy(j).wait_recv()
        to_groups(j, lambda r: z_recv[j][r], 0)

    def group_first(j):
        to_groups(j, lambda r: z_send[j, r], 1)

    def section_second(j):
        group_copy(j, 0, GROUPS - 1).wait_recv()
        for k in range(REQ):
            z_send[j, k] = x_recv[j][rows[1, k]]
        section_copy(j).start()

    find(1, section)
    states(0)
    states(1)
    pl.semaphore_wait(barrier, 2 + (GROUPS - 1) + len(near))
    pl.semaphore_signal(
        relay, inc=1, device_id=(section, group, lax.rem(tensor + 2, TENSORS)), device_id_type=MESH
    )
    section_copy(2).start()
    group_first(0)
    section_copy(3).start()
    group_first(1)
    states(2)
    group_first(4)
    group_first(5)
    states(3)
    section_copy(6).start()
    section_copy(7).start()
    find(0, behind)
    group_second(2)
    section_second(0)

    z_copy.wait()

    def gate(r, _):
        value = mixed[r] * silu(z_v[r].astype(F32))
        mixed[r] = value
        acc = jnp.zeros((LEN, 128), F32)
        for p in range(WIDTH // 128):
            part = value[:, p * 128:(p + 1) * 128]
            acc = acc + part * part
        squares[pl.ds(pl.multiple_of(r * LEN, LEN), LEN), :] = acc
        return 0

    lax.fori_loop(0, REQ, gate, 0)

    def exchange(which):
        copies = []
        for d in range(1, TENSORS):
            copy = pltpu.make_async_remote_copy(
                pack.at[which], got.at[which, d], t_sem.at[2 * which, d], t_sem.at[2 * which + 1, d],
                device_id=(section, group, lax.rem(tensor + d, TENSORS)), device_id_type=MESH,
            )
            copy.start()
            copies.append(copy)
        return copies

    pack[...] = jnp.zeros_like(pack)
    row8 = iota((8, 128), 0)
    packed = jnp.zeros((8, 128), F32)
    for q in range(4):
        sums = jnp.sum(jnp.transpose(squares[q * 128:(q + 1) * 128, :]), axis=0, keepdims=True)
        packed = jnp.where(row8 == q, sums, packed)
    pack[0] = packed
    pl.semaphore_wait(relay, 1)
    pre_copies = exchange(0)

    turn[...] = jnp.zeros_like(turn)
    for s in range(REQ):
        turn[s * STEPS:(s + 1) * STEPS, 0:HEADS] = dec_dt[s]
    lane_d = iota((1, 128), 1)
    dec_step = softplus(turn[0:REQ * STEPS, :] + from_scalars(bias, lane_d, HEADS))
    dec_dec = jnp.exp(-from_scalars(rate, lane_d, HEADS) * dec_step)
    both = jnp.concatenate([dec_step, dec_dec], axis=0)
    heads_wide = (iota((128, WIDTH), 0) == iota((128, WIDTH), 1) // 64).astype(F32).astype(BF16)
    wide = sum(dot(term, heads_wide) for term in three_terms(both))
    pairs = REQ // 2
    dec_inject[...] = wide[0:REQ * STEPS].reshape(pairs, 8, WIDTH)
    dec_decay[...] = wide[REQ * STEPS:2 * REQ * STEPS].reshape(pairs, 8, WIDTH)
    skip_wide = from_scalars(skip, iota((1, WIDTH), 1) // 64, HEADS)
    for s in range(REQ):
        at = slice((s % 2) * STEPS, (s % 2) * STEPS + STEPS)
        x_f = dec_x[s].astype(F32)
        dec_inject[s // 2, at, :] = dec_inject[s // 2, at, :] * x_f
        dec_skip[s // 2, at, :] = skip_wide * x_f
        dec_gate[s // 2, at, :] = silu(dec_z[s].astype(F32))
    turn[...] = jnp.zeros_like(turn)
    for s in range(REQ):
        turn[s * STEPS:(s + 1) * STEPS, 0:STATE] = dec_b[s].astype(F32)
        turn[s * STEPS:(s + 1) * STEPS, STATE:2 * STATE] = dec_c[s].astype(F32)
    cols_t = jnp.transpose(turn[0:128, :])[0:2 * STATE]
    pick = (lax.rem(iota((128, WIDTH), 0), 8) == iota((128, WIDTH), 1) // 128).astype(F32).astype(BF16)
    lane_p = iota((2 * STATE, 128), 1) // 8

    for p in range(pairs):
        dec_cols[p] = dot(jnp.where(lane_p == p, cols_t, 0.0).astype(BF16), pick)
    dec_squares[...] = jnp.zeros_like(dec_squares)

    state_out = []

    def decode(j):
        if j in GROUP_FIRST:
            section_copy(j).wait_recv()
        else:
            group_copy(j, 0, GROUPS - 1).wait_recv()
        cols = slice(j * PART, (j + 1) * PART)

        def pair(p, _):
            y = jnp.zeros((8, PART), F32)
            for i in range(2):
                if j in GROUP_FIRST:
                    state = z_recv[j][2 * p + i]
                else:
                    state = x_recv[j][rows[0, 2 * p + i]]
                for t in range(STEPS):
                    q = i * STEPS + t
                    b_col = dec_cols[p, 0:STATE, q * 128:(q + 1) * 128]
                    c_col = dec_cols[p, STATE:2 * STATE, q * 128:(q + 1) * 128]
                    state = state * dec_decay[p, q:q + 1, cols] + b_col * dec_inject[p, q:q + 1, cols]
                    y = jnp.where(row8 == q, jnp.sum(state * c_col, axis=0, keepdims=True), y)
                staged[2 * p + i, :, cols] = state
            value = (y + dec_skip[p, :, cols]) * dec_gate[p, :, cols]
            dec_gated[p, :, cols] = value
            at = pl.ds(pl.multiple_of(p * 8, 8), 8)
            dec_squares[at, :] = dec_squares[at, :] + value * value
            return 0

        lax.fori_loop(0, pairs, pair, 0)
        copy = pltpu.make_async_copy(
            staged.at[:, :, pl.ds(j * PART, PART)], state_hbm.at[:, :, pl.ds(j * PART, PART)],
            local_sem.at[blocks + 1 + j],
        )
        copy.start()
        state_out.append(copy)

    def summed(which, copies):
        for copy in copies:
            copy.wait_recv()
        acc = pack[which]
        for d in range(1, TENSORS):
            acc = acc + got[which, d]
        return lax.rsqrt(acc / CHAN + EPS)

    gain_row = gain[...]
    pre_out = []
    group_second(3)
    section_second(1)
    group_second(6)
    section_second(4)
    group_second(7)
    section_second(5)
    decode(0)
    decode(2)
    decode(1)
    decode(3)
    decode(4)
    scale = summed(0, pre_copies)
    lane_t = iota((8, 128), 1)
    req8 = row8 * 4 + lane_t // LEN
    scale = jnp.where(lax.rem(lane_t, LEN) < from_scalars(lengths, req8, REQ), scale, 0.0)
    for q in range(4):
        squares[q * 128:(q + 1) * 128, :] = jnp.transpose(
            jnp.broadcast_to(scale[q:q + 1, :], (128, 128))
        )

    def finish(r, _):
        col = squares[pl.ds(pl.multiple_of(r * LEN, LEN), LEN), :]
        for p in range(WIDTH // 128):
            at = slice(p * 128, (p + 1) * 128)
            pre_v[r, :, at] = (mixed[r, :, at] * col * gain_row[:, at]).astype(BF16)
        return 0

    lax.fori_loop(0, REQ, finish, 0)
    copy = pltpu.make_async_copy(pre_v, pre_hbm, local_sem.at[blocks + 1 + PARTS])
    copy.start()
    pre_out.append(copy)
    decode(6)
    decode(5)
    decode(7)

    sums = jnp.sum(jnp.transpose(dec_squares[...]), axis=0, keepdims=True)
    pack[1] = jnp.broadcast_to(sums, (8, 128))
    dec_copies = exchange(1)
    scale = summed(1, dec_copies)
    column = jnp.transpose(jnp.broadcast_to(scale[0:1, :], (128, 128)))
    for p in range(pairs):
        col = column[p * 8:(p + 1) * 8, :]
        for c in range(WIDTH // 128):
            at = slice(c * 128, (c + 1) * 128)
            value = (dec_gated[p, :, at] * col * gain_row[:, at]).astype(BF16)
            dec_v[2 * p, :, at] = value[0:STEPS]
            dec_v[2 * p + 1, :, at] = value[STEPS:2 * STEPS]
    dec_copy = pltpu.make_async_copy(dec_v, dec_hbm, local_sem.at[blocks + 2 + PARTS])
    dec_copy.start()

    for j in range(PARTS):
        section_copy(j).wait_send()
        group_copy(j, 0, GROUPS - 1).wait_send()
    for copy in pre_copies + dec_copies:
        copy.wait_send()
    for copy in state_out + pre_out:
        copy.wait()
    dec_copy.wait()


def place(pre, dec, state, pre_hbm, dec_hbm, state_hbm, pre_v, dec_v, state_v, in_sem, out_sem):
    parts = [(dec, dec_v, dec_hbm)]
    for k in range(PLACE_PARTS):
        some = pl.ds(k * (REQ // PLACE_PARTS), REQ // PLACE_PARTS)
        parts.append((pre.at[some], pre_v.at[some], pre_hbm.at[some]))
        parts.append((state.at[some], state_v.at[some], state_hbm.at[some]))
    arriving = [pltpu.make_async_copy(a, b, in_sem.at[k]) for k, (a, b, _) in enumerate(parts)]
    leaving = [pltpu.make_async_copy(b, c, out_sem.at[k]) for k, (_, b, c) in enumerate(parts)]
    for copy in arriving:
        copy.start()
    for copy, then in zip(arriving, leaving):
        copy.wait()
        then.start()
    for copy in leaving:
        copy.wait()


def local(
    x_pre, z_pre, b_pre, c_pre, dt_pre, lengths, owner,
    dec_x, dec_z, dec_b, dec_c, dec_dt, decay_rate, dt_bias, skip, norm_gain,
):
    smem = pl.BlockSpec(memory_space=pltpu.SMEM)
    vmem = pl.BlockSpec(memory_space=pltpu.VMEM)
    anywhere = pl.BlockSpec(memory_space=pl.ANY)
    tokens = (REQ, LEN, WIDTH)
    steps = (REQ // 2, 8, WIDTH)
    scratch = [
        pltpu.VMEM(tokens, BF16),
        pltpu.VMEM(tokens, BF16),
        pltpu.VMEM((REQ * HEADS, 128), F32),
        pltpu.VMEM((REQ, LEN + STATE, 3 * LEN), BF16),
        pltpu.VMEM((REQ, 2 * LEN, 2 * HEADS), BF16),
        pltpu.VMEM(tokens, F32),
        pltpu.VMEM((REQ * LEN, 128), F32),
        pltpu.VMEM((PARTS, REQ, STATE, PART), F32),
        pltpu.VMEM((PARTS, 2 * GROUPS, STATE, PART), F32),
        pltpu.VMEM((REQ, STATE, WIDTH), F32),
        pltpu.VMEM(tokens, BF16),
        pltpu.VMEM((REQ, STEPS, WIDTH), BF16),
        pltpu.VMEM(steps, F32),
        pltpu.VMEM(steps, F32),
        pltpu.VMEM(steps, F32),
        pltpu.VMEM(steps, F32),
        pltpu.VMEM((REQ // 2, 2 * STATE, WIDTH), F32),
        pltpu.VMEM(steps, F32),
        pltpu.VMEM((128, 128), F32),
        pltpu.VMEM((2, 8, 128), F32),
        pltpu.VMEM((2, TENSORS, 8, 128), F32),
        pltpu.SMEM((2, 2 * GROUPS), jnp.int32),
        pltpu.SMEM((2, REQ), jnp.int32),
        pltpu.SemaphoreType.DMA((WIDTH // BLOCK + 3 + PARTS,)),
        pltpu.SemaphoreType.DMA((2, PARTS)),
        pltpu.SemaphoreType.DMA((2, PARTS)),
        pltpu.SemaphoreType.DMA((4, TENSORS)),
        pltpu.SemaphoreType.REGULAR,
    ]
    scratch += [pltpu.VMEM((REQ, STATE, PART), F32) for _ in range(PARTS)]
    scratch += [pltpu.VMEM((2 * GROUPS, STATE, PART), F32) for _ in range(PARTS)]
    outs = pl.pallas_call(
        kernel,
        out_shape=(
            jax.ShapeDtypeStruct(tokens, BF16),
            jax.ShapeDtypeStruct((REQ, STEPS, WIDTH), BF16),
            jax.ShapeDtypeStruct((REQ, STATE, WIDTH), F32),
        ),
        in_specs=[smem] * 5 + [vmem] * 9 + [anywhere] * 2,
        out_specs=(anywhere, anywhere, anywhere),
        scratch_shapes=scratch,
        compiler_params=pltpu.CompilerParams(
            collective_id=0, has_side_effects=True, vmem_limit_bytes=56 << 20
        ),
    )(
        lengths, owner, decay_rate, dt_bias, skip,
        jnp.transpose(b_pre, (0, 2, 1)), jnp.transpose(c_pre, (0, 2, 1)), jnp.transpose(dt_pre, (0, 2, 1)),
        dec_x, dec_z, dec_b, dec_c, dec_dt, norm_gain.reshape(1, WIDTH),
        x_pre, z_pre,
    )
    return pl.pallas_call(
        place,
        out_shape=tuple(jax.ShapeDtypeStruct(v.shape, v.dtype) for v in outs),
        in_specs=[anywhere] * 3,
        out_specs=(anywhere,) * 3,
        scratch_shapes=[pltpu.VMEM(v.shape, v.dtype) for v in outs] + [
            pltpu.SemaphoreType.DMA((2 * PLACE_PARTS + 1,)) for _ in range(2)
        ],
        compiler_params=pltpu.CompilerParams(vmem_limit_bytes=56 << 20),
    )(*outs)


def solution(mesh):
    cell = ("section", "group")
    return jax.shard_map(
        local,
        mesh=mesh,
        in_specs=(
            P(cell, None, "tensor"), P(cell, None, "tensor"), P(cell, None, None), P(cell, None, None),
            P(cell, None, "tensor"), P(cell), P(), P(cell, None, "tensor"), P(cell, None, "tensor"),
            P(cell, None, None), P(cell, None, None), P(cell, None, "tensor"),
            P("tensor"), P("tensor"), P("tensor"), P("tensor"),
        ),
        out_specs=(P(cell, None, "tensor"),) * 3,
        check_vma=False,
    )
```

```python
import functools

import jax
import jax.numpy as jnp
from jax import lax
from jax.experimental import pallas as pl
from jax.experimental.pallas import tpu as pltpu
from jax.sharding import PartitionSpec as P

CHAN = 8192
EPS = 1e-05
MESH = pl.DeviceIdType.MESH
F32 = jnp.float32
BF16 = jnp.bfloat16

REQ = 16
LEN = 32
STATE = 16
HEADS = 16
WIDTH = 1024
STEPS = 4
SIDE = 4
GROUPS = 16
SECTIONS = 4
TENSORS = 8
PARTS = 8
PART = WIDTH // PARTS
BLOCK = 256
GROUP_FIRST = (0, 1, 4, 5)
PLACE_PARTS = 4
UNROLL = 8


def iota(shape, dim):
    return lax.broadcasted_iota(jnp.int32, shape, dim)


def softplus(v):
    return jnp.maximum(v, 0.0) + jnp.log1p(jnp.exp(-jnp.abs(v)))


def silu(v):
    return v / (1.0 + jnp.exp(-v))


def two_terms(v):
    high = v.astype(BF16)
    return high, (v - high.astype(F32)).astype(BF16)


def three_terms(v):
    high = v.astype(BF16)
    rest = v - high.astype(F32)
    mid = rest.astype(BF16)
    return high, mid, (rest - mid.astype(F32)).astype(BF16)


def dot(a, b):
    return jnp.dot(a, b, preferred_element_type=F32)


def from_scalars(ref, where_index, count):
    acc = jnp.zeros(where_index.shape, ref.dtype)
    for k in range(count):
        acc = jnp.where(where_index == k, ref[k], acc)
    return acc


def kernel(
    lengths, owner, rate, bias, skip,
    b_t, c_t, dt_t, dec_x, dec_z, dec_b, dec_c, dec_dt, gain,
    x_hbm, z_hbm,
    pre_hbm, dec_hbm, state_hbm,
    *scratch,
):
    (x_v, z_v, turn, lhs, expand_lhs, mixed, squares, z_send, x_send, staged, pre_v,
     dec_v, dec_decay, dec_inject, dec_skip, dec_gate, dec_cols, dec_gated, dec_squares,
     pack, got, source, rows, local_sem, z_sem, x_sem, t_sem, relay) = scratch[:28]
    z_recv = scratch[28:28 + PARTS]
    x_recv = scratch[28 + PARTS:28 + 2 * PARTS]

    section = lax.axis_index("section")
    group = lax.axis_index("group")
    tensor = lax.axis_index("tensor")
    gx, gy = group // SIDE, lax.rem(group, SIDE)
    ahead = lax.rem(section + 1, SECTIONS)
    behind = lax.rem(section + SECTIONS - 1, SECTIONS)

    def farther_first(a):
        return lax.rem(2 + a + a // 2 + 2 * (a // 3), SIDE)

    def group_at(d):
        by_x, by_y = farther_first(d // SIDE), farther_first(lax.rem(d, SIDE))
        return lax.rem(gx + by_x, SIDE) * SIDE + lax.rem(gy + by_y, SIDE)

    blocks = WIDTH // BLOCK
    x_copies = []
    for k in range(blocks):
        cols = pl.ds(k * BLOCK, BLOCK)
        copy = pltpu.make_async_copy(x_hbm.at[:, :, cols], x_v.at[:, :, cols], local_sem.at[k])
        copy.start()
        x_copies.append(copy)
    z_copy = pltpu.make_async_copy(z_hbm, z_v, local_sem.at[blocks])
    z_copy.start()

    barrier = pltpu.get_barrier_semaphore()
    for to in (ahead, behind):
        pl.semaphore_signal(barrier, inc=1, device_id=(to, group, tensor), device_id_type=MESH)
    for d in range(GROUPS - 1):
        pl.semaphore_signal(barrier, inc=1, device_id=(section, group_at(d), tensor), device_id_type=MESH)
    core = lax.rem(tensor, 2)
    near = [tensor + 1 - 2 * core]
    for by in (2, TENSORS - 2):
        near += [lax.rem(tensor - core + by, TENSORS) + c for c in range(2)]
    for to in near:
        pl.semaphore_signal(barrier, inc=1, device_id=(section, group, to), device_id_type=MESH)

    turn[...] = jnp.zeros_like(turn)
    turn[:, 0:LEN] = dt_t[...].reshape(REQ * HEADS, LEN)
    logits = jnp.transpose(turn[...])[0:LEN]
    lane = iota((1, REQ * HEADS), 1)
    head_of, req_of = lax.rem(lane, HEADS), lane // HEADS
    live = iota((LEN, REQ * HEADS), 0) < from_scalars(lengths, req_of, REQ)
    step = jnp.where(live, softplus(logits + from_scalars(bias, head_of, HEADS)), 0.0)
    fall = from_scalars(rate, head_of, HEADS) * step
    lower = (iota((LEN, LEN), 0) >= iota((LEN, LEN), 1)).astype(F32).astype(BF16)
    total = sum(dot(lower, term) for term in three_terms(fall))
    shrink = jnp.exp(-total)
    grow = jnp.exp(total) * step

    turn[:, 0:LEN] = c_t[...].reshape(REQ * STATE, LEN).astype(F32)
    c_tok = jnp.transpose(turn[...])[0:LEN]
    spread = (lax.rem(iota((LEN, 3 * LEN), 1), LEN) == iota((LEN, 3 * LEN), 0)).astype(F32).astype(BF16)
    b_rep = dot(b_t[...].reshape(REQ * STATE, LEN), spread)
    lane3 = iota((LEN, 3 * LEN), 1)
    middle = (lane3 >= LEN) & (lane3 < 2 * LEN)
    causal = iota((LEN, 3 * LEN), 0) >= lax.rem(lane3, LEN)
    lane128 = iota((LEN, 128), 1) // HEADS
    half_reqs = 128 // HEADS
    for r in range(REQ):
        half = slice((r // half_reqs) * 128, (r // half_reqs) * 128 + 128)
        mine = lane128 == r % half_reqs
        for at, values in ((0, grow), (LEN, shrink)):
            high, low = two_terms(values[:, r * HEADS:(r + 1) * HEADS])
            expand_lhs[r, at:at + LEN, 0:HEADS] = high
            expand_lhs[r, at:at + LEN, HEADS:2 * HEADS] = low
        gram = dot(jnp.where(mine, c_tok[:, half], 0.0).astype(BF16), b_rep[half].astype(BF16))
        high = gram.astype(BF16).astype(F32)
        lhs[r, 0:LEN, :] = jnp.where(causal, jnp.where(middle, gram - high, high), 0.0).astype(BF16)
        lhs[r, LEN:LEN + STATE, :] = jnp.where(
            middle[0:STATE], 0.0, b_rep[r * STATE:(r + 1) * STATE]
        ).astype(BF16)

    def states(k):
        x_copies[k].wait()
        cols = slice(k * BLOCK, (k + 1) * BLOCK)
        head_rows = lax.rem(iota((2 * HEADS, BLOCK), 0), HEADS)
        head_cols = iota((2 * HEADS, BLOCK), 1) // 64 + k * (BLOCK // 64)
        expand = (head_rows == head_cols).astype(F32).astype(BF16)
        skip_row = from_scalars(skip, iota((1, BLOCK), 1) // 64 + k * (BLOCK // 64), HEADS)

        def prefill(i, _):
            first = i * UNROLL
            wides = dot(expand_lhs[pl.ds(first, UNROLL)].reshape(UNROLL * 2 * LEN, 2 * HEADS), expand)
            for sub in range(UNROLL):
                r = first + sub
                wide = wides[sub * 2 * LEN:(sub + 1) * 2 * LEN]
                x_f = x_v[r, :, cols].astype(F32)
                high, low = two_terms(x_f * wide[0:LEN])
                res = dot(lhs[r], jnp.concatenate([high, high, low], axis=0))
                mixed[r, :, cols] = res[0:LEN] * wide[LEN:2 * LEN] + skip_row * x_f
                final = res[LEN:LEN + STATE] * wide[2 * LEN - 1:2 * LEN]
                for p in range(BLOCK // PART):
                    z_send[k * (BLOCK // PART) + p, r] = final[:, p * PART:(p + 1) * PART]
            return 0

        lax.fori_loop(0, REQ // UNROLL, prefill, 0)

    def section_copy(j):
        return pltpu.make_async_remote_copy(
            z_send.at[j], z_recv[j], z_sem.at[0, j], z_sem.at[1, j],
            device_id=(ahead, group, tensor), device_id_type=MESH,
        )

    def find(at, from_section):
        first_request = (from_section * GROUPS + group) * REQ

        def find_source(h, _):
            low, high = jnp.int32(REQ - 1), jnp.int32(0)
            for r in range(REQ):
                is_it = owner[first_request + r] == h
                low = jnp.minimum(low, jnp.where(is_it, r, REQ - 1))
                high = jnp.maximum(high, jnp.where(is_it, r, 0))
            source[at, 2 * h] = low
            source[at, 2 * h + 1] = high
            return 0

        def find_rows(cell, carry):
            place, found = carry[0], carry[1:]
            count = jnp.int32(0)
            for r in range(REQ):
                is_it = owner[(from_section * GROUPS + cell) * REQ + r] == group
                count = count + jnp.where(is_it, 1, 0)
            has = jnp.where(count > 0, 1, 0)
            spot = jnp.where(count > 0, place, -1)
            return (place + has,) + tuple(jnp.where(spot == j, cell, v) for j, v in enumerate(found))

        lax.fori_loop(0, GROUPS, find_source, 0)
        found = lax.fori_loop(0, GROUPS, find_rows, (jnp.int32(0),) * (1 + REQ // 2))[1:]
        for j, cell in enumerate(found):
            rows[at, 2 * j] = 2 * cell
            rows[at, 2 * j + 1] = 2 * cell + 1

    def group_copy(j, d, count=1):
        rows_of = 2 * count
        return pltpu.make_async_remote_copy(
            x_send.at[j, pl.ds(2 * d, rows_of)],
            x_recv[j].at[pl.ds(2 * group if count == 1 else 2 * d, rows_of)],
            x_sem.at[0, j], x_sem.at[1, j],
            device_id=(section, group_at(d), tensor), device_id_type=MESH,
        )

    def to_groups(j, state_of, at):
        for p in range(2):
            x_recv[j][2 * group + p] = state_of(source[at, 2 * group + p])

        def fill(d, _):
            h = group_at(d)
            for p in range(2):
                x_send[j, 2 * d + p] = state_of(source[at, 2 * h + p])
            group_copy(j, d).start()
            return 0

        lax.fori_loop(0, GROUPS - 1, fill, 0)

    def group_second(j):
        section_copy(j).wait_recv()
        to_groups(j, lambda r: z_recv[j][r], 0)

    def group_first(j):
        to_groups(j, lambda r: z_send[j, r], 1)

    def section_second(j):
        group_copy(j, 0, GROUPS - 1).wait_recv()
        for k in range(REQ):
            z_send[j, k] = x_recv[j][rows[1, k]]
        section_copy(j).start()

    find(1, section)
    states(0)
    states(1)
    pl.semaphore_wait(barrier, 2 + (GROUPS - 1) + len(near))
    pl.semaphore_signal(
        relay, inc=1, device_id=(section, group, lax.rem(tensor + 2, TENSORS)), device_id_type=MESH
    )
    section_copy(2).start()
    group_first(0)
    section_copy(3).start()
    group_first(1)
    states(2)
    group_first(4)
    group_first(5)
    states(3)
    section_copy(6).start()
    section_copy(7).start()
    find(0, behind)
    group_second(2)
    section_second(0)

    z_copy.wait()

    def gate(r, _):
        value = mixed[r] * silu(z_v[r].astype(F32))
        mixed[r] = value
        acc = jnp.zeros((LEN, 128), F32)
        for p in range(WIDTH // 128):
            part = value[:, p * 128:(p + 1) * 128]
            acc = acc + part * part
        squares[pl.ds(pl.multiple_of(r * LEN, LEN), LEN), :] = acc
        return 0

    lax.fori_loop(0, REQ, gate, 0)

    def exchange(which):
        copies = []
        used = 4 if which == 0 else 1
        for d in range(1, TENSORS):
            copy = pltpu.make_async_remote_copy(
                pack.at[which, pl.ds(0, used)], got.at[which, d, pl.ds(0, used)], t_sem.at[2 * which, d], t_sem.at[2 * which + 1, d],
                device_id=(section, group, lax.rem(tensor + d, TENSORS)), device_id_type=MESH,
            )
            copy.start()
            copies.append(copy)
        return copies

    pack[...] = jnp.zeros_like(pack)
    row8 = iota((8, 128), 0)
    packed = jnp.zeros((8, 128), F32)
    for q in range(4):
        sums = jnp.sum(jnp.transpose(squares[q * 128:(q + 1) * 128, :]), axis=0, keepdims=True)
        packed = jnp.where(row8 == q, sums, packed)
    pack[0] = packed
    pl.semaphore_wait(relay, 1)
    pre_copies = exchange(0)

    turn[...] = jnp.zeros_like(turn)
    for s in range(REQ):
        turn[s * STEPS:(s + 1) * STEPS, 0:HEADS] = dec_dt[s]
    lane_d = iota((1, 128), 1)
    dec_step = softplus(turn[0:REQ * STEPS, :] + from_scalars(bias, lane_d, HEADS))
    dec_dec = jnp.exp(-from_scalars(rate, lane_d, HEADS) * dec_step)
    both = jnp.concatenate([dec_step, dec_dec], axis=0)
    heads_wide = (iota((128, WIDTH), 0) == iota((128, WIDTH), 1) // 64).astype(F32).astype(BF16)
    wide = sum(dot(term, heads_wide) for term in three_terms(both))
    pairs = REQ // 2
    dec_inject[...] = wide[0:REQ * STEPS].reshape(pairs, 8, WIDTH)
    dec_decay[...] = wide[REQ * STEPS:2 * REQ * STEPS].reshape(pairs, 8, WIDTH)
    skip_wide = from_scalars(skip, iota((1, WIDTH), 1) // 64, HEADS)
    for s in range(REQ):
        at = slice((s % 2) * STEPS, (s % 2) * STEPS + STEPS)
        x_f = dec_x[s].astype(F32)
        dec_inject[s // 2, at, :] = dec_inject[s // 2, at, :] * x_f
        dec_skip[s // 2, at, :] = skip_wide * x_f
        dec_gate[s // 2, at, :] = silu(dec_z[s].astype(F32))
    turn[...] = jnp.zeros_like(turn)
    for s in range(REQ):
        turn[s * STEPS:(s + 1) * STEPS, 0:STATE] = dec_b[s].astype(F32)
        turn[s * STEPS:(s + 1) * STEPS, STATE:2 * STATE] = dec_c[s].astype(F32)
    cols_t = jnp.transpose(turn[0:128, :])[0:2 * STATE]
    pick = (lax.rem(iota((128, WIDTH), 0), 8) == iota((128, WIDTH), 1) // 128).astype(F32).astype(BF16)
    lane_p = iota((2 * STATE, 128), 1) // 8

    for p in range(pairs):
        dec_cols[p] = dot(jnp.where(lane_p == p, cols_t, 0.0).astype(BF16), pick)
    dec_squares[...] = jnp.zeros_like(dec_squares)

    state_out = []

    def decode(j):
        if j in GROUP_FIRST:
            section_copy(j).wait_recv()
        else:
            group_copy(j, 0, GROUPS - 1).wait_recv()
        cols = slice(j * PART, (j + 1) * PART)

        def pair(p, _):
            y = jnp.zeros((8, PART), F32)
            for i in range(2):
                if j in GROUP_FIRST:
                    state = z_recv[j][2 * p + i]
                else:
                    state = x_recv[j][rows[0, 2 * p + i]]
                for t in range(STEPS):
                    q = i * STEPS + t
                    b_col = dec_cols[p, 0:STATE, q * 128:(q + 1) * 128]
                    c_col = dec_cols[p, STATE:2 * STATE, q * 128:(q + 1) * 128]
                    state = state * dec_decay[p, q:q + 1, cols] + b_col * dec_inject[p, q:q + 1, cols]
                    y = jnp.where(row8 == q, jnp.sum(state * c_col, axis=0, keepdims=True), y)
                staged[2 * p + i, :, cols] = state
            value = (y + dec_skip[p, :, cols]) * dec_gate[p, :, cols]
            dec_gated[p, :, cols] = value
            at = pl.ds(pl.multiple_of(p * 8, 8), 8)
            dec_squares[at, :] = dec_squares[at, :] + value * value
            return 0

        lax.fori_loop(0, pairs, pair, 0)
        copy = pltpu.make_async_copy(
            staged.at[:, :, pl.ds(j * PART, PART)], state_hbm.at[:, :, pl.ds(j * PART, PART)],
            local_sem.at[blocks + 1 + j],
        )
        copy.start()
        state_out.append(copy)

    def summed(which, copies):
        for copy in copies:
            copy.wait_recv()
        acc = pack[which]
        used = 4 if which == 0 else 1
        acc = acc[0:used]
        for d in range(1, TENSORS):
            acc = acc + got[which, d, 0:used]
        return lax.rsqrt(acc / CHAN + EPS)

    gain_row = gain[...]
    pre_out = []
    group_second(3)
    section_second(1)
    group_second(6)
    section_second(4)
    group_second(7)
    section_second(5)
    decode(0)
    decode(2)
    decode(1)
    decode(3)
    decode(4)
    scale = summed(0, pre_copies)
    lane_t = iota((4, 128), 1)
    req8 = iota((4, 128), 0) * 4 + lane_t // LEN
    scale = jnp.where(lax.rem(lane_t, LEN) < from_scalars(lengths, req8, REQ), scale, 0.0)
    for q in range(4):
        squares[q * 128:(q + 1) * 128, :] = jnp.transpose(
            jnp.broadcast_to(scale[q:q + 1, :], (128, 128))
        )

    def finish(r, _):
        col = squares[pl.ds(pl.multiple_of(r * LEN, LEN), LEN), :]
        for p in range(WIDTH // 128):
            at = slice(p * 128, (p + 1) * 128)
            pre_v[r, :, at] = (mixed[r, :, at] * col * gain_row[:, at]).astype(BF16)
        return 0

    lax.fori_loop(0, REQ, finish, 0)
    copy = pltpu.make_async_copy(pre_v, pre_hbm, local_sem.at[blocks + 1 + PARTS])
    copy.start()
    pre_out.append(copy)
    decode(6)
    decode(5)
    decode(7)

    sums = jnp.sum(jnp.transpose(dec_squares[...]), axis=0, keepdims=True)
    pack[1] = jnp.broadcast_to(sums, (8, 128))
    dec_copies = exchange(1)
    scale = summed(1, dec_copies)
    column = jnp.transpose(jnp.broadcast_to(scale, (128, 128)))
    for p in range(pairs):
        col = column[p * 8:(p + 1) * 8, :]
        for c in range(WIDTH // 128):
            at = slice(c * 128, (c + 1) * 128)
            value = (dec_gated[p, :, at] * col * gain_row[:, at]).astype(BF16)
            dec_v[2 * p, :, at] = value[0:STEPS]
            dec_v[2 * p + 1, :, at] = value[STEPS:2 * STEPS]
    dec_copy = pltpu.make_async_copy(dec_v, dec_hbm, local_sem.at[blocks + 2 + PARTS])
    dec_copy.start()

    for j in range(PARTS):
        section_copy(j).wait_send()
        group_copy(j, 0, GROUPS - 1).wait_send()
    for copy in pre_copies + dec_copies:
        copy.wait_send()
    for copy in state_out + pre_out:
        copy.wait()
    dec_copy.wait()


def place(pre, dec, state, pre_hbm, dec_hbm, state_hbm, pre_v, dec_v, state_v, in_sem, out_sem):
    parts = [(dec, dec_v, dec_hbm)]
    for k in range(PLACE_PARTS):
        some = pl.ds(k * (REQ // PLACE_PARTS), REQ // PLACE_PARTS)
        parts.append((pre.at[some], pre_v.at[some], pre_hbm.at[some]))
        parts.append((state.at[some], state_v.at[some], state_hbm.at[some]))
    arriving = [pltpu.make_async_copy(a, b, in_sem.at[k]) for k, (a, b, _) in enumerate(parts)]
    leaving = [pltpu.make_async_copy(b, c, out_sem.at[k]) for k, (_, b, c) in enumerate(parts)]
    for copy in arriving:
        copy.start()
    for copy, then in zip(arriving, leaving):
        copy.wait()
        then.start()
    for copy in leaving:
        copy.wait()


def local(
    x_pre, z_pre, b_pre, c_pre, dt_pre, lengths, owner,
    dec_x, dec_z, dec_b, dec_c, dec_dt, decay_rate, dt_bias, skip, norm_gain,
):
    smem = pl.BlockSpec(memory_space=pltpu.SMEM)
    vmem = pl.BlockSpec(memory_space=pltpu.VMEM)
    anywhere = pl.BlockSpec(memory_space=pl.ANY)
    tokens = (REQ, LEN, WIDTH)
    steps = (REQ // 2, 8, WIDTH)
    scratch = [
        pltpu.VMEM(tokens, BF16),
        pltpu.VMEM(tokens, BF16),
        pltpu.VMEM((REQ * HEADS, 128), F32),
        pltpu.VMEM((REQ, LEN + STATE, 3 * LEN), BF16),
        pltpu.VMEM((REQ, 2 * LEN, 2 * HEADS), BF16),
        pltpu.VMEM(tokens, F32),
        pltpu.VMEM((REQ * LEN, 128), F32),
        pltpu.VMEM((PARTS, REQ, STATE, PART), F32),
        pltpu.VMEM((PARTS, 2 * GROUPS, STATE, PART), F32),
        pltpu.VMEM((REQ, STATE, WIDTH), F32),
        pltpu.VMEM(tokens, BF16),
        pltpu.VMEM((REQ, STEPS, WIDTH), BF16),
        pltpu.VMEM(steps, F32),
        pltpu.VMEM(steps, F32),
        pltpu.VMEM(steps, F32),
        pltpu.VMEM(steps, F32),
        pltpu.VMEM((REQ // 2, 2 * STATE, WIDTH), F32),
        pltpu.VMEM(steps, F32),
        pltpu.VMEM((128, 128), F32),
        pltpu.VMEM((2, 8, 128), F32),
        pltpu.VMEM((2, TENSORS, 8, 128), F32),
        pltpu.SMEM((2, 2 * GROUPS), jnp.int32),
        pltpu.SMEM((2, REQ), jnp.int32),
        pltpu.SemaphoreType.DMA((WIDTH // BLOCK + 3 + PARTS,)),
        pltpu.SemaphoreType.DMA((2, PARTS)),
        pltpu.SemaphoreType.DMA((2, PARTS)),
        pltpu.SemaphoreType.DMA((4, TENSORS)),
        pltpu.SemaphoreType.REGULAR,
    ]
    scratch += [pltpu.VMEM((REQ, STATE, PART), F32) for _ in range(PARTS)]
    scratch += [pltpu.VMEM((2 * GROUPS, STATE, PART), F32) for _ in range(PARTS)]
    outs = pl.pallas_call(
        kernel,
        out_shape=(
            jax.ShapeDtypeStruct(tokens, BF16),
            jax.ShapeDtypeStruct((REQ, STEPS, WIDTH), BF16),
            jax.ShapeDtypeStruct((REQ, STATE, WIDTH), F32),
        ),
        in_specs=[smem] * 5 + [vmem] * 9 + [anywhere] * 2,
        out_specs=(anywhere, anywhere, anywhere),
        scratch_shapes=scratch,
        compiler_params=pltpu.CompilerParams(
            collective_id=0, has_side_effects=True, vmem_limit_bytes=56 << 20
        ),
    )(
        lengths, owner, decay_rate, dt_bias, skip,
        jnp.transpose(b_pre, (0, 2, 1)), jnp.transpose(c_pre, (0, 2, 1)), jnp.transpose(dt_pre, (0, 2, 1)),
        dec_x, dec_z, dec_b, dec_c, dec_dt, norm_gain.reshape(1, WIDTH),
        x_pre, z_pre,
    )
    return pl.pallas_call(
        place,
        out_shape=tuple(jax.ShapeDtypeStruct(v.shape, v.dtype) for v in outs),
        in_specs=[anywhere] * 3,
        out_specs=(anywhere,) * 3,
        scratch_shapes=[pltpu.VMEM(v.shape, v.dtype) for v in outs] + [
            pltpu.SemaphoreType.DMA((2 * PLACE_PARTS + 1,)) for _ in range(2)
        ],
        compiler_params=pltpu.CompilerParams(vmem_limit_bytes=56 << 20),
    )(*outs)


def solution(mesh):
    cell = ("section", "group")
    return jax.shard_map(
        local,
        mesh=mesh,
        in_specs=(
            P(cell, None, "tensor"), P(cell, None, "tensor"), P(cell, None, None), P(cell, None, None),
            P(cell, None, "tensor"), P(cell), P(), P(cell, None, "tensor"), P(cell, None, "tensor"),
            P(cell, None, None), P(cell, None, None), P(cell, None, "tensor"),
            P("tensor"), P("tensor"), P("tensor"), P("tensor"),
        ),
        out_specs=(P(cell, None, "tensor"),) * 3,
        check_vma=False,
    )
```

```python
import functools

import jax
import jax.numpy as jnp
from jax import lax
from jax.experimental import pallas as pl
from jax.experimental.pallas import tpu as pltpu
from jax.sharding import PartitionSpec as P

CHAN = 8192
EPS = 1e-05
MESH = pl.DeviceIdType.MESH
F32 = jnp.float32
BF16 = jnp.bfloat16

REQ = 16
LEN = 32
STATE = 16
HEADS = 16
WIDTH = 1024
STEPS = 4
SIDE = 4
GROUPS = 16
SECTIONS = 4
TENSORS = 8
PARTS = 8
PART = WIDTH // PARTS
BLOCK = 256
GROUP_FIRST = (0, 1, 4, 5)
PLACE_PARTS = 4
UNROLL = 8


def iota(shape, dim):
    return lax.broadcasted_iota(jnp.int32, shape, dim)


def softplus(v):
    return jnp.maximum(v, 0.0) + jnp.log1p(jnp.exp(-jnp.abs(v)))


def silu(v):
    return v / (1.0 + jnp.exp(-v))


def two_terms(v):
    high = v.astype(BF16)
    return high, (v - high.astype(F32)).astype(BF16)


def three_terms(v):
    high = v.astype(BF16)
    rest = v - high.astype(F32)
    mid = rest.astype(BF16)
    return high, mid, (rest - mid.astype(F32)).astype(BF16)


def dot(a, b):
    return jnp.dot(a, b, preferred_element_type=F32)


def from_scalars(ref, where_index, count):
    acc = jnp.zeros(where_index.shape, ref.dtype)
    for k in range(count):
        acc = jnp.where(where_index == k, ref[k], acc)
    return acc


def kernel(
    lengths, owner, rate, bias, skip,
    b_t, c_t, dt_t, dec_x, dec_z, dec_b, dec_c, dec_dt, gain,
    x_hbm, z_hbm,
    pre_hbm, dec_hbm, state_hbm,
    *scratch,
):
    (x_v, z_v, turn, lhs, expand_lhs, mixed, squares, z_send, x_send, staged, pre_v,
     dec_v, dec_decay, dec_inject, dec_skip, dec_gate, dec_cols, dec_gated, dec_squares,
     pack, got, source, rows, local_sem, z_sem, x_sem, t_sem, relay) = scratch[:28]
    z_recv = scratch[28:28 + PARTS]
    x_recv = scratch[28 + PARTS:28 + 2 * PARTS]

    section = lax.axis_index("section")
    group = lax.axis_index("group")
    tensor = lax.axis_index("tensor")
    gx, gy = group // SIDE, lax.rem(group, SIDE)
    ahead = lax.rem(section + 1, SECTIONS)
    behind = lax.rem(section + SECTIONS - 1, SECTIONS)

    def farther_first(a):
        return lax.rem(2 + a + a // 2 + 2 * (a // 3), SIDE)

    def group_at(d):
        by_x, by_y = farther_first(d // SIDE), farther_first(lax.rem(d, SIDE))
        return lax.rem(gx + by_x, SIDE) * SIDE + lax.rem(gy + by_y, SIDE)

    blocks = WIDTH // BLOCK
    x_copies = []
    for k in range(blocks):
        cols = pl.ds(k * BLOCK, BLOCK)
        copy = pltpu.make_async_copy(x_hbm.at[:, :, cols], x_v.at[:, :, cols], local_sem.at[k])
        copy.start()
        x_copies.append(copy)
    z_copy = pltpu.make_async_copy(z_hbm, z_v, local_sem.at[blocks])
    z_copy.start()

    barrier = pltpu.get_barrier_semaphore()
    for to in (ahead, behind):
        pl.semaphore_signal(barrier, inc=1, device_id=(to, group, tensor), device_id_type=MESH)
    for d in range(GROUPS - 1):
        pl.semaphore_signal(barrier, inc=1, device_id=(section, group_at(d), tensor), device_id_type=MESH)
    core = lax.rem(tensor, 2)
    near = [tensor + 1 - 2 * core]
    for by in (2, TENSORS - 2):
        near += [lax.rem(tensor - core + by, TENSORS) + c for c in range(2)]
    for to in near:
        pl.semaphore_signal(barrier, inc=1, device_id=(section, group, to), device_id_type=MESH)

    turn[...] = jnp.zeros_like(turn)
    turn[:, 0:LEN] = dt_t[...].reshape(REQ * HEADS, LEN)
    logits = jnp.transpose(turn[...])[0:LEN]
    lane = iota((1, REQ * HEADS), 1)
    head_of, req_of = lax.rem(lane, HEADS), lane // HEADS
    live = iota((LEN, REQ * HEADS), 0) < from_scalars(lengths, req_of, REQ)
    step = jnp.where(live, softplus(logits + from_scalars(bias, head_of, HEADS)), 0.0)
    fall = from_scalars(rate, head_of, HEADS) * step
    lower = (iota((LEN, LEN), 0) >= iota((LEN, LEN), 1)).astype(F32).astype(BF16)
    total = sum(dot(lower, term) for term in three_terms(fall))
    shrink = jnp.exp(-total)
    grow = jnp.exp(total) * step

    turn[:, 0:LEN] = c_t[...].reshape(REQ * STATE, LEN).astype(F32)
    c_tok = jnp.transpose(turn[...])[0:LEN]
    spread = (lax.rem(iota((LEN, 3 * LEN), 1), LEN) == iota((LEN, 3 * LEN), 0)).astype(F32).astype(BF16)
    b_rep = dot(b_t[...].reshape(REQ * STATE, LEN), spread)
    lane3 = iota((LEN, 3 * LEN), 1)
    middle = (lane3 >= LEN) & (lane3 < 2 * LEN)
    causal = iota((LEN, 3 * LEN), 0) >= lax.rem(lane3, LEN)
    lane128 = iota((LEN, 128), 1) // HEADS
    half_reqs = 128 // HEADS
    for r in range(REQ):
        half = slice((r // half_reqs) * 128, (r // half_reqs) * 128 + 128)
        mine = lane128 == r % half_reqs
        for at, values in ((0, grow), (LEN, shrink)):
            high, low = two_terms(values[:, r * HEADS:(r + 1) * HEADS])
            expand_lhs[r, at:at + LEN, 0:HEADS] = high
            expand_lhs[r, at:at + LEN, HEADS:2 * HEADS] = low
        gram = dot(jnp.where(mine, c_tok[:, half], 0.0).astype(BF16), b_rep[half].astype(BF16))
        high = gram.astype(BF16).astype(F32)
        lhs[r, 0:LEN, :] = jnp.where(causal, jnp.where(middle, gram - high, high), 0.0).astype(BF16)
        lhs[r, LEN:LEN + STATE, :] = jnp.where(
            middle[0:STATE], 0.0, b_rep[r * STATE:(r + 1) * STATE]
        ).astype(BF16)

    def states(k):
        x_copies[k].wait()
        cols = slice(k * BLOCK, (k + 1) * BLOCK)
        head_rows = lax.rem(iota((2 * HEADS, BLOCK), 0), HEADS)
        head_cols = iota((2 * HEADS, BLOCK), 1) // 64 + k * (BLOCK // 64)
        expand = (head_rows == head_cols).astype(F32).astype(BF16)
        skip_row = from_scalars(skip, iota((1, BLOCK), 1) // 64 + k * (BLOCK // 64), HEADS)

        def prefill(i, _):
            first = i * UNROLL
            wides = dot(expand_lhs[pl.ds(first, UNROLL)].reshape(UNROLL * 2 * LEN, 2 * HEADS), expand)
            for sub in range(UNROLL):
                r = first + sub
                wide = wides[sub * 2 * LEN:(sub + 1) * 2 * LEN]
                x_f = x_v[r, :, cols].astype(F32)
                high, low = two_terms(x_f * wide[0:LEN])
                res = dot(lhs[r], jnp.concatenate([high, high, low], axis=0))
                mixed[r, :, cols] = res[0:LEN] * wide[LEN:2 * LEN] + skip_row * x_f
                final = res[LEN:LEN + STATE] * wide[2 * LEN - 1:2 * LEN]
                for p in range(BLOCK // PART):
                    z_send[k * (BLOCK // PART) + p, r] = final[:, p * PART:(p + 1) * PART]
            return 0

        lax.fori_loop(0, REQ // UNROLL, prefill, 0)

    def section_copy(j):
        return pltpu.make_async_remote_copy(
            z_send.at[j], z_recv[j], z_sem.at[0, j], z_sem.at[1, j],
            device_id=(ahead, group, tensor), device_id_type=MESH,
        )

    def find(at, from_section):
        first_request = (from_section * GROUPS + group) * REQ

        def find_source(h, _):
            low, high = jnp.int32(REQ - 1), jnp.int32(0)
            for r in range(REQ):
                is_it = owner[first_request + r] == h
                low = jnp.minimum(low, jnp.where(is_it, r, REQ - 1))
                high = jnp.maximum(high, jnp.where(is_it, r, 0))
            source[at, 2 * h] = low
            source[at, 2 * h + 1] = high
            return 0

        def find_rows(cell, carry):
            place, found = carry[0], carry[1:]
            count = jnp.int32(0)
            for r in range(REQ):
                is_it = owner[(from_section * GROUPS + cell) * REQ + r] == group
                count = count + jnp.where(is_it, 1, 0)
            has = jnp.where(count > 0, 1, 0)
            spot = jnp.where(count > 0, place, -1)
            return (place + has,) + tuple(jnp.where(spot == j, cell, v) for j, v in enumerate(found))

        lax.fori_loop(0, GROUPS, find_source, 0)
        found = lax.fori_loop(0, GROUPS, find_rows, (jnp.int32(0),) * (1 + REQ // 2))[1:]
        for j, cell in enumerate(found):
            rows[at, 2 * j] = 2 * cell
            rows[at, 2 * j + 1] = 2 * cell + 1

    def group_copy(j, d, count=1):
        rows_of = 2 * count
        return pltpu.make_async_remote_copy(
            x_send.at[j, pl.ds(2 * d, rows_of)],
            x_recv[j].at[pl.ds(2 * group if count == 1 else 2 * d, rows_of)],
            x_sem.at[0, j], x_sem.at[1, j],
            device_id=(section, group_at(d), tensor), device_id_type=MESH,
        )

    def to_groups(j, state_of, at):
        for p in range(2):
            x_recv[j][2 * group + p] = state_of(source[at, 2 * group + p])

        def fill(d, _):
            h = group_at(d)
            for p in range(2):
                x_send[j, 2 * d + p] = state_of(source[at, 2 * h + p])
            group_copy(j, d).start()
            return 0

        lax.fori_loop(0, GROUPS - 1, fill, 0)

    def group_second(j):
        section_copy(j).wait_recv()
        to_groups(j, lambda r: z_recv[j][r], 0)

    def group_first(j):
        to_groups(j, lambda r: z_send[j, r], 1)

    def section_second(j):
        group_copy(j, 0, GROUPS - 1).wait_recv()
        for k in range(REQ):
            z_send[j, k] = x_recv[j][rows[1, k]]
        section_copy(j).start()

    find(1, section)
    states(0)
    pl.semaphore_wait(barrier, 2 + (GROUPS - 1) + len(near))
    pl.semaphore_signal(
        relay, inc=1, device_id=(section, group, lax.rem(tensor + 2, TENSORS)), device_id_type=MESH
    )
    group_first(0)
    group_first(1)
    states(1)
    section_copy(2).start()
    section_copy(3).start()
    states(2)
    group_first(4)
    group_first(5)
    states(3)
    section_copy(6).start()
    section_copy(7).start()
    find(0, behind)
    group_second(2)
    section_second(0)

    z_copy.wait()

    def gate(r, _):
        value = mixed[r] * silu(z_v[r].astype(F32))
        mixed[r] = value
        acc = jnp.zeros((LEN, 128), F32)
        for p in range(WIDTH // 128):
            part = value[:, p * 128:(p + 1) * 128]
            acc = acc + part * part
        squares[pl.ds(pl.multiple_of(r * LEN, LEN), LEN), :] = acc
        return 0

    lax.fori_loop(0, REQ, gate, 0)

    def exchange(which):
        copies = []
        used = 4 if which == 0 else 1
        for d in range(1, TENSORS):
            copy = pltpu.make_async_remote_copy(
                pack.at[which, pl.ds(0, used)], got.at[which, d, pl.ds(0, used)], t_sem.at[2 * which, d], t_sem.at[2 * which + 1, d],
                device_id=(section, group, lax.rem(tensor + d, TENSORS)), device_id_type=MESH,
            )
            copy.start()
            copies.append(copy)
        return copies

    pack[...] = jnp.zeros_like(pack)
    row8 = iota((8, 128), 0)
    packed = jnp.zeros((8, 128), F32)
    for q in range(4):
        sums = jnp.sum(jnp.transpose(squares[q * 128:(q + 1) * 128, :]), axis=0, keepdims=True)
        packed = jnp.where(row8 == q, sums, packed)
    pack[0] = packed
    pl.semaphore_wait(relay, 1)
    pre_copies = exchange(0)

    turn[...] = jnp.zeros_like(turn)
    for s in range(REQ):
        turn[s * STEPS:(s + 1) * STEPS, 0:HEADS] = dec_dt[s]
    lane_d = iota((1, 128), 1)
    dec_step = softplus(turn[0:REQ * STEPS, :] + from_scalars(bias, lane_d, HEADS))
    dec_dec = jnp.exp(-from_scalars(rate, lane_d, HEADS) * dec_step)
    both = jnp.concatenate([dec_step, dec_dec], axis=0)
    heads_wide = (iota((128, WIDTH), 0) == iota((128, WIDTH), 1) // 64).astype(F32).astype(BF16)
    wide = sum(dot(term, heads_wide) for term in three_terms(both))
    pairs = REQ // 2
    dec_inject[...] = wide[0:REQ * STEPS].reshape(pairs, 8, WIDTH)
    dec_decay[...] = wide[REQ * STEPS:2 * REQ * STEPS].reshape(pairs, 8, WIDTH)
    skip_wide = from_scalars(skip, iota((1, WIDTH), 1) // 64, HEADS)
    for s in range(REQ):
        at = slice((s % 2) * STEPS, (s % 2) * STEPS + STEPS)
        x_f = dec_x[s].astype(F32)
        dec_inject[s // 2, at, :] = dec_inject[s // 2, at, :] * x_f
        dec_skip[s // 2, at, :] = skip_wide * x_f
        dec_gate[s // 2, at, :] = silu(dec_z[s].astype(F32))
    turn[...] = jnp.zeros_like(turn)
    for s in range(REQ):
        turn[s * STEPS:(s + 1) * STEPS, 0:STATE] = dec_b[s].astype(F32)
        turn[s * STEPS:(s + 1) * STEPS, STATE:2 * STATE] = dec_c[s].astype(F32)
    cols_t = jnp.transpose(turn[0:128, :])[0:2 * STATE]
    pick = (lax.rem(iota((128, WIDTH), 0), 8) == iota((128, WIDTH), 1) // 128).astype(F32).astype(BF16)
    lane_p = iota((2 * STATE, 128), 1) // 8

    for p in range(pairs):
        dec_cols[p] = dot(jnp.where(lane_p == p, cols_t, 0.0).astype(BF16), pick)
    dec_squares[...] = jnp.zeros_like(dec_squares)

    state_out = []

    def decode(j):
        if j in GROUP_FIRST:
            section_copy(j).wait_recv()
        else:
            group_copy(j, 0, GROUPS - 1).wait_recv()
        cols = slice(j * PART, (j + 1) * PART)

        def pair(p, _):
            y = jnp.zeros((8, PART), F32)
            for i in range(2):
                if j in GROUP_FIRST:
                    state = z_recv[j][2 * p + i]
                else:
                    state = x_recv[j][rows[0, 2 * p + i]]
                for t in range(STEPS):
                    q = i * STEPS + t
                    b_col = dec_cols[p, 0:STATE, q * 128:(q + 1) * 128]
                    c_col = dec_cols[p, STATE:2 * STATE, q * 128:(q + 1) * 128]
                    state = state * dec_decay[p, q:q + 1, cols] + b_col * dec_inject[p, q:q + 1, cols]
                    y = jnp.where(row8 == q, jnp.sum(state * c_col, axis=0, keepdims=True), y)
                staged[2 * p + i, :, cols] = state
            value = (y + dec_skip[p, :, cols]) * dec_gate[p, :, cols]
            dec_gated[p, :, cols] = value
            at = pl.ds(pl.multiple_of(p * 8, 8), 8)
            dec_squares[at, :] = dec_squares[at, :] + value * value
            return 0

        lax.fori_loop(0, pairs, pair, 0)
        copy = pltpu.make_async_copy(
            staged.at[:, :, pl.ds(j * PART, PART)], state_hbm.at[:, :, pl.ds(j * PART, PART)],
            local_sem.at[blocks + 1 + j],
        )
        copy.start()
        state_out.append(copy)

    def summed(which, copies):
        for copy in copies:
            copy.wait_recv()
        acc = pack[which]
        used = 4 if which == 0 else 1
        acc = acc[0:used]
        for d in range(1, TENSORS):
            acc = acc + got[which, d, 0:used]
        return lax.rsqrt(acc / CHAN + EPS)

    gain_row = gain[...]
    pre_out = []
    group_second(3)
    section_second(1)
    group_second(6)
    section_second(4)
    group_second(7)
    section_second(5)
    decode(0)
    decode(2)
    decode(1)
    decode(3)
    decode(4)
    scale = summed(0, pre_copies)
    lane_t = iota((4, 128), 1)
    req8 = iota((4, 128), 0) * 4 + lane_t // LEN
    scale = jnp.where(lax.rem(lane_t, LEN) < from_scalars(lengths, req8, REQ), scale, 0.0)
    for q in range(4):
        squares[q * 128:(q + 1) * 128, :] = jnp.transpose(
            jnp.broadcast_to(scale[q:q + 1, :], (128, 128))
        )

    def finish(r, _):
        col = squares[pl.ds(pl.multiple_of(r * LEN, LEN), LEN), :]
        for p in range(WIDTH // 128):
            at = slice(p * 128, (p + 1) * 128)
            pre_v[r, :, at] = (mixed[r, :, at] * col * gain_row[:, at]).astype(BF16)
        return 0

    lax.fori_loop(0, REQ, finish, 0)
    copy = pltpu.make_async_copy(pre_v, pre_hbm, local_sem.at[blocks + 1 + PARTS])
    copy.start()
    pre_out.append(copy)
    decode(6)
    decode(5)
    decode(7)

    sums = jnp.sum(jnp.transpose(dec_squares[...]), axis=0, keepdims=True)
    pack[1] = jnp.broadcast_to(sums, (8, 128))
    dec_copies = exchange(1)
    scale = summed(1, dec_copies)
    column = jnp.transpose(jnp.broadcast_to(scale, (128, 128)))
    for p in range(pairs):
        col = column[p * 8:(p + 1) * 8, :]
        for c in range(WIDTH // 128):
            at = slice(c * 128, (c + 1) * 128)
            value = (dec_gated[p, :, at] * col * gain_row[:, at]).astype(BF16)
            dec_v[2 * p, :, at] = value[0:STEPS]
            dec_v[2 * p + 1, :, at] = value[STEPS:2 * STEPS]
    dec_copy = pltpu.make_async_copy(dec_v, dec_hbm, local_sem.at[blocks + 2 + PARTS])
    dec_copy.start()

    for j in range(PARTS):
        section_copy(j).wait_send()
        group_copy(j, 0, GROUPS - 1).wait_send()
    for copy in pre_copies + dec_copies:
        copy.wait_send()
    for copy in state_out + pre_out:
        copy.wait()
    dec_copy.wait()


def place(pre, dec, state, pre_hbm, dec_hbm, state_hbm, pre_v, dec_v, state_v, in_sem, out_sem):
    parts = [(dec, dec_v, dec_hbm)]
    for k in range(PLACE_PARTS):
        some = pl.ds(k * (REQ // PLACE_PARTS), REQ // PLACE_PARTS)
        parts.append((pre.at[some], pre_v.at[some], pre_hbm.at[some]))
        parts.append((state.at[some], state_v.at[some], state_hbm.at[some]))
    arriving = [pltpu.make_async_copy(a, b, in_sem.at[k]) for k, (a, b, _) in enumerate(parts)]
    leaving = [pltpu.make_async_copy(b, c, out_sem.at[k]) for k, (_, b, c) in enumerate(parts)]
    for copy in arriving:
        copy.start()
    for copy, then in zip(arriving, leaving):
        copy.wait()
        then.start()
    for copy in leaving:
        copy.wait()


def local(
    x_pre, z_pre, b_pre, c_pre, dt_pre, lengths, owner,
    dec_x, dec_z, dec_b, dec_c, dec_dt, decay_rate, dt_bias, skip, norm_gain,
):
    smem = pl.BlockSpec(memory_space=pltpu.SMEM)
    vmem = pl.BlockSpec(memory_space=pltpu.VMEM)
    anywhere = pl.BlockSpec(memory_space=pl.ANY)
    tokens = (REQ, LEN, WIDTH)
    steps = (REQ // 2, 8, WIDTH)
    scratch = [
        pltpu.VMEM(tokens, BF16),
        pltpu.VMEM(tokens, BF16),
        pltpu.VMEM((REQ * HEADS, 128), F32),
        pltpu.VMEM((REQ, LEN + STATE, 3 * LEN), BF16),
        pltpu.VMEM((REQ, 2 * LEN, 2 * HEADS), BF16),
        pltpu.VMEM(tokens, F32),
        pltpu.VMEM((REQ * LEN, 128), F32),
        pltpu.VMEM((PARTS, REQ, STATE, PART), F32),
        pltpu.VMEM((PARTS, 2 * GROUPS, STATE, PART), F32),
        pltpu.VMEM((REQ, STATE, WIDTH), F32),
        pltpu.VMEM(tokens, BF16),
        pltpu.VMEM((REQ, STEPS, WIDTH), BF16),
        pltpu.VMEM(steps, F32),
        pltpu.VMEM(steps, F32),
        pltpu.VMEM(steps, F32),
        pltpu.VMEM(steps, F32),
        pltpu.VMEM((REQ // 2, 2 * STATE, WIDTH), F32),
        pltpu.VMEM(steps, F32),
        pltpu.VMEM((128, 128), F32),
        pltpu.VMEM((2, 8, 128), F32),
        pltpu.VMEM((2, TENSORS, 8, 128), F32),
        pltpu.SMEM((2, 2 * GROUPS), jnp.int32),
        pltpu.SMEM((2, REQ), jnp.int32),
        pltpu.SemaphoreType.DMA((WIDTH // BLOCK + 3 + PARTS,)),
        pltpu.SemaphoreType.DMA((2, PARTS)),
        pltpu.SemaphoreType.DMA((2, PARTS)),
        pltpu.SemaphoreType.DMA((4, TENSORS)),
        pltpu.SemaphoreType.REGULAR,
    ]
    scratch += [pltpu.VMEM((REQ, STATE, PART), F32) for _ in range(PARTS)]
    scratch += [pltpu.VMEM((2 * GROUPS, STATE, PART), F32) for _ in range(PARTS)]
    outs = pl.pallas_call(
        kernel,
        out_shape=(
            jax.ShapeDtypeStruct(tokens, BF16),
            jax.ShapeDtypeStruct((REQ, STEPS, WIDTH), BF16),
            jax.ShapeDtypeStruct((REQ, STATE, WIDTH), F32),
        ),
        in_specs=[smem] * 5 + [vmem] * 9 + [anywhere] * 2,
        out_specs=(anywhere, anywhere, anywhere),
        scratch_shapes=scratch,
        compiler_params=pltpu.CompilerParams(
            collective_id=0, has_side_effects=True, vmem_limit_bytes=56 << 20
        ),
    )(
        lengths, owner, decay_rate, dt_bias, skip,
        jnp.transpose(b_pre, (0, 2, 1)), jnp.transpose(c_pre, (0, 2, 1)), jnp.transpose(dt_pre, (0, 2, 1)),
        dec_x, dec_z, dec_b, dec_c, dec_dt, norm_gain.reshape(1, WIDTH),
        x_pre, z_pre,
    )
    return pl.pallas_call(
        place,
        out_shape=tuple(jax.ShapeDtypeStruct(v.shape, v.dtype) for v in outs),
        in_specs=[anywhere] * 3,
        out_specs=(anywhere,) * 3,
        scratch_shapes=[pltpu.VMEM(v.shape, v.dtype) for v in outs] + [
            pltpu.SemaphoreType.DMA((2 * PLACE_PARTS + 1,)) for _ in range(2)
        ],
        compiler_params=pltpu.CompilerParams(vmem_limit_bytes=56 << 20),
    )(*outs)


def solution(mesh):
    cell = ("section", "group")
    return jax.shard_map(
        local,
        mesh=mesh,
        in_specs=(
            P(cell, None, "tensor"), P(cell, None, "tensor"), P(cell, None, None), P(cell, None, None),
            P(cell, None, "tensor"), P(cell), P(), P(cell, None, "tensor"), P(cell, None, "tensor"),
            P(cell, None, None), P(cell, None, None), P(cell, None, "tensor"),
            P("tensor"), P("tensor"), P("tensor"), P("tensor"),
        ),
        out_specs=(P(cell, None, "tensor"),) * 3,
        check_vma=False,
    )
```
